32 devices in a mesh: groups: 2 (over x), space: 16 (over z, y, core).
Axes of the slice: x: 2, y: 2, z: 4, core: 2. Of those that a mesh axis runs over, the one named last changes fastest.
Arguments:
- atom_features: bfloat16 [288, 32, 256], P(('groups', 'space')), parts along dimension 0, may hold values from -6 to 6
- offsets: bfloat16 [288, 3, 32], P(('groups', 'space')), parts along dimension 0, may hold values from 0 to 1
- counts: int32 [288], P(('groups', 'space')), parts along dimension 0, may hold values from 8 to 32, as said below
- radial_weight: bfloat16 [4, 256, 256], replicated, may hold values from -0.375 to 0.375
- charge_weight: bfloat16 [256, 256], replicated, may hold values from -0.375 to 0.375
- wave_filter: float32 [4, 256], replicated, may hold values from -5 to 5
- wavevectors: int32 [3, 1024], replicated, may hold values from -4 to 25, as said below
Outputs:
- updated: bfloat16 [288, 32, 256], P(('groups', 'space')), parts along dimension 0
The draws below stay inside these ranges and needn't reach their ends.
There are 2 independent parts, one for each index of `groups`. The reference program is written for one: setup_inputs(seed, part) draws one part's arguments, and reference() takes and returns one part's arrays. A program takes and returns all parts, laid end to end along the dimension named above; an argument that names none is the same for every part. Nothing has to cross between parts.
Inputs may be any that keep to these rules, and one draw needn't show every extreme that they name: Cell c holds its atoms in its first counts[c] slots; in every draw some cell is full. `wavevectors`: the 1024 columns are distinct index triples from one half of the lattice: no column is zero or the negative of another; the first two indices lie in -4 to 4 and the third in 0 to 25, and where the third is 0 the first is above 0, or the first is 0 and the second above 0.
All inputs are finite; a program needn't handle non-finite values.
Results may differ from the reference program's by a relative error of at most 0.005.
Values may be sent and summed in bfloat16 or wider, within the bound.
No kernel may reach another device: no remote copies, remote signals or barrier semaphores. Data moves between devices by JAX's collectives and lax.ppermute only.
A program may use at most 64 MiB of HBM per device.

```python
import math
import jax
import jax.numpy as jnp
from jax import lax

H = 256
K = 1024
NUM_BASIS = 4
CAP = 32
GRID = 3
NCELL = 144
N_SPACE = 16


def draw_counts(key, part):
    first_key, second_key = jax.random.split(jax.random.fold_in(key, 17))
    drawn_counts = jax.random.randint(first_key, (NCELL,), CAP // 4, CAP + 1)
    full_cell = jax.random.randint(second_key, (), 0, NCELL)
    return jnp.where(jnp.arange(NCELL) == full_cell, CAP, drawn_counts).astype(jnp.int32)


def draw_wavevectors(key, part):
    layer_depth = 25
    plane_count = 81
    first_key, second_key = jax.random.split(jax.random.fold_in(key, 29))
    candidate_total = 40 + layer_depth * plane_count
    forced_index = 40 + (layer_depth - 1) * plane_count
    picked = jax.random.permutation(first_key, candidate_total - 1)[:K - 1].astype(jnp.int32)
    picked = picked + (picked >= forced_index).astype(jnp.int32)
    chosen = jnp.concatenate([jnp.full((1,), forced_index, jnp.int32), picked])
    chosen = chosen[jax.random.permutation(second_key, K)]
    in_plane = chosen < 40
    remainder = chosen - 40
    layer_index = jnp.where(in_plane, 0, 1 + remainder // plane_count)
    flat_plane = jnp.where(in_plane, 41 + chosen, remainder % plane_count)
    index_x = flat_plane // 9 - 4
    index_y = flat_plane % 9 - 4
    return jnp.stack([index_x, index_y, layer_index]).astype(jnp.int32)


def level_of(rng, extent, cuts, smallest, top_value):
    loudness, own = 1.0, jax.random.fold_in(rng, 6)
    for dim, shards_of in cuts:
        heights = jnp.exp(jax.random.uniform(jax.random.fold_in(own, dim), (shards_of,), jnp.float32, smallest / len(cuts), top_value / len(cuts)))
        loudness = loudness * jnp.repeat(heights, extent[dim] // shards_of).reshape([-1 if axis == dim else 1 for axis in range(len(extent))])
    return loudness


def scatter_about(rng, shape, deviation, limit, cuts=(), held_as=jnp.bfloat16):
    level = level_of(rng, shape, cuts, -0.22, 0.18) if cuts else 1.0
    array = jax.random.normal(rng, shape, jnp.float32) * deviation * level
    return jnp.minimum(jnp.maximum(array, -limit), limit).astype(held_as)


def setup_inputs(seed: int = 0, part: int = 0) -> dict:
    seeds = jax.random.split(jax.random.key(seed), 8)
    own_keys = jax.random.split(jax.random.fold_in(seeds[7], part), 8)
    atom_features = scatter_about(own_keys[0], (NCELL, CAP, H), 1.0, 6.0, ((0, 16),))
    offsets = jnp.clip(1.0 * jax.random.uniform(own_keys[1], (NCELL, 3, CAP), jnp.float32) ** level_of(own_keys[1], (NCELL, 3, CAP), ((0, 16),), -0.2, 0.2), 0.0, 1.0).astype(jnp.bfloat16)
    counts = draw_counts(jax.random.fold_in(jax.random.fold_in(seeds[7], part), 71), part)
    radial_weight = scatter_about(seeds[3], (NUM_BASIS, H, H), H ** -0.5, 0.375)
    charge_weight = scatter_about(seeds[4], (H, H), H ** -0.5, 0.375)
    wave_filter = scatter_about(seeds[5], (NUM_BASIS, H), 1.0, 5.0, (), jnp.float32)
    wavevectors = draw_wavevectors(jax.random.fold_in(seeds[7], 71), part)
    return {"atom_features": atom_features, "offsets": offsets, "counts": counts, "radial_weight": radial_weight, "charge_weight": charge_weight, "wave_filter": wave_filter, "wavevectors": wavevectors}


CUTOFF = 1.0
block_rows = 512

def cell_geometry(near_count, cell_slots):
    columns = jnp.arange(near_count * cell_slots, dtype=jnp.int32)
    return (columns // cell_slots, columns % cell_slots)

def pair_tile(own_coords, near_coords, near_cell, near_slot, cell_index, layer_cells, basis_index, basis_count):
    own_x = cell_index // GRID
    own_y = cell_index % GRID
    layer_of = near_cell // layer_cells
    within = near_cell % layer_cells
    shift_x = ((within // GRID - own_x + 1) % GRID - 1).astype(jnp.float32)
    shift_y = ((within % GRID - own_y + 1) % GRID - 1).astype(jnp.float32)
    shift_z = (layer_of - 1).astype(jnp.float32)
    own_pos = own_coords.astype(jnp.float32)
    near_pos = near_coords.astype(jnp.float32)
    delta_x = (shift_x + near_pos[0])[None, :] - own_pos[0][:, None]
    delta_y = (shift_y + near_pos[1])[None, :] - own_pos[1][:, None]
    delta_z = (shift_z + near_pos[2])[None, :] - own_pos[2][:, None]
    radius = jnp.sqrt(delta_x * delta_x + delta_y * delta_y + delta_z * delta_z)
    smooth = jnp.where(radius < CUTOFF, 0.5 * (jnp.cos(math.pi * radius / CUTOFF) + 1.0), 0.0)
    centre = (basis_index + 0.5) * CUTOFF / basis_count
    scaled = (radius - centre) * (basis_count / CUTOFF)
    slot_ids = jnp.arange(own_pos.shape[1], dtype=jnp.int32)
    itself = (near_cell == layer_cells + cell_index)[None, :] & (near_slot[None, :] == slot_ids[:, None])
    return jnp.where(itself, 0.0, jnp.exp(-(scaled * scaled)) * smooth).astype(jnp.bfloat16)

def wave_numbers(wave_rows, layers_total):
    two_pi = 2.0 * math.pi
    wave_float = wave_rows.astype(jnp.float32)
    along_x = two_pi * wave_float[0] / GRID
    along_y = two_pi * wave_float[1] / GRID
    along_z = two_pi * wave_float[2] / layers_total
    return (along_x, along_y, along_z)

def phase_table(positions, wave_rows, layers_total):
    along_x, along_y, along_z = wave_numbers(wave_rows, layers_total)
    return positions[0][:, None] * along_x[None, :] + positions[1][:, None] * along_y[None, :] + positions[2][:, None] * along_z[None, :]

def structure_terms(positions, charges, wave_rows, layers_total):
    row_count = wave_rows.shape[1]
    feature_width = charges.shape[1]
    block_size = block_rows if row_count > block_rows and row_count % block_rows == 0 else row_count
    pieces = jnp.transpose(wave_rows.reshape(3, row_count // block_size, block_size), (1, 0, 2))

    def one_block(wave_block):
        phases = phase_table(positions, wave_block, layers_total)
        cosine = jnp.cos(phases).astype(jnp.bfloat16)
        sine_part = jnp.sin(phases).astype(jnp.bfloat16)
        real_part = lax.dot_general(cosine, charges, (((0,), (0,)), ((), ())), preferred_element_type=jnp.float32)
        imag_part = lax.dot_general(sine_part, charges, (((0,), (0,)), ((), ())), preferred_element_type=jnp.float32)
        return jnp.concatenate([real_part, imag_part], axis=1)
    return lax.map(one_block, pieces).reshape(row_count, 2 * feature_width)

def filter_rows(structure, wave_rows, layers_total, wave_filter):
    along_x, along_y, along_z = wave_numbers(wave_rows, layers_total)
    magnitude = jnp.sqrt(along_x * along_x + along_y * along_y + along_z * along_z)
    centres = 3.0 * jnp.arange(wave_filter.shape[0], dtype=jnp.float32)
    offset_k = (magnitude[:, None] - centres[None, :]) / 3.0
    basis_rows = jnp.exp(-(offset_k * offset_k))
    gain_rows = jnp.dot(basis_rows, wave_filter, precision=lax.Precision.HIGHEST, preferred_element_type=jnp.float32)
    return (structure * jnp.concatenate([gain_rows, gain_rows], axis=1)).astype(jnp.bfloat16)

def add_inverse(running, filtered, wave_rows, positions, layers_total):
    row_count = filtered.shape[0]
    feature_width = filtered.shape[1] // 2
    block_size = block_rows if row_count > block_rows and row_count % block_rows == 0 else row_count
    block_count = row_count // block_size
    factor_blocks = filtered.reshape(block_count, block_size, 2 * feature_width)
    wave_blocks = jnp.transpose(wave_rows.reshape(3, block_count, block_size), (1, 0, 2))

    def one_block(summed, block_item):
        factors, wave_block = block_item
        phases = phase_table(positions, wave_block, layers_total)
        cosine = jnp.cos(phases).astype(jnp.bfloat16)
        sine_part = jnp.sin(phases).astype(jnp.bfloat16)
        summed = summed + jnp.dot(cosine, factors[:, :feature_width], preferred_element_type=jnp.float32)
        summed = summed + jnp.dot(sine_part, factors[:, feature_width:], preferred_element_type=jnp.float32)
        return (summed, None)
    outcome = lax.scan(one_block, running, (factor_blocks, wave_blocks))
    return outcome[0]

def reference(atom_features, offsets, counts, radial_weight, charge_weight, wave_filter, wavevectors):
    layer_cells = GRID * GRID
    layers_total = N_SPACE
    total_cells = layer_cells * layers_total
    near_count = 3 * layer_cells
    slot_ids = jnp.arange(CAP, dtype=jnp.int32)
    live_mask = (slot_ids[None, :] < counts[:, None]).astype(jnp.float32)
    masked = (atom_features.astype(jnp.float32) * live_mask[:, :, None]).astype(jnp.bfloat16)
    masked_flat = masked.reshape(total_cells * CAP, H)
    values = jnp.stack([jnp.dot(masked_flat, radial_weight[basis_index], preferred_element_type=jnp.float32).astype(jnp.bfloat16) for basis_index in range(NUM_BASIS)])
    values = values.reshape(NUM_BASIS, layers_total, layer_cells * CAP, H)
    layer_offsets = offsets.reshape(layers_total, layer_cells, 3, CAP)
    near_cell, near_slot = cell_geometry(near_count, CAP)
    cell_ids = jnp.arange(layer_cells, dtype=jnp.int32)

    def layer_short(layer_index):
        below_layer = (layer_index - 1) % layers_total
        above_layer = (layer_index + 1) % layers_total
        near_offsets = jnp.concatenate([layer_offsets[below_layer], layer_offsets[layer_index], layer_offsets[above_layer]], axis=0)
        near_coords = jnp.transpose(near_offsets, (1, 0, 2)).reshape(3, near_count * CAP)
        near_values = jnp.concatenate([values[:, below_layer], values[:, layer_index], values[:, above_layer]], axis=1)

        def cell_short(cell_index):
            own_coords = layer_offsets[layer_index, cell_index]
            running = jnp.zeros((CAP, H), jnp.float32)
            for basis_index in range(NUM_BASIS):
                pair_weights = pair_tile(own_coords, near_coords, near_cell, near_slot, cell_index, layer_cells, basis_index, NUM_BASIS)
                running = running + jnp.dot(pair_weights, near_values[basis_index], preferred_element_type=jnp.float32)
            return running
        return lax.map(cell_short, cell_ids)
    short_sum = lax.map(layer_short, jnp.arange(layers_total, dtype=jnp.int32)).reshape(total_cells, CAP, H)
    cell_all = jnp.arange(total_cells, dtype=jnp.int32)
    within = cell_all % layer_cells
    base_x = (within // GRID).astype(jnp.float32)
    base_y = (within % GRID).astype(jnp.float32)
    base_z = (cell_all // layer_cells).astype(jnp.float32)
    coords = offsets.astype(jnp.float32)
    positions = jnp.stack([(base_x[:, None] + coords[:, 0, :]).reshape(-1), (base_y[:, None] + coords[:, 1, :]).reshape(-1), (base_z[:, None] + coords[:, 2, :]).reshape(-1)])
    charges = jnp.dot(masked_flat, charge_weight, preferred_element_type=jnp.float32).astype(jnp.bfloat16)
    structure = structure_terms(positions, charges, wavevectors, layers_total)
    filtered = filter_rows(structure, wavevectors, layers_total, wave_filter)
    reciprocal = add_inverse(jnp.zeros((total_cells * CAP, H), jnp.float32), filtered, wavevectors, positions, layers_total)
    short_scaled = short_sum * (1.0 / math.sqrt(CAP))
    recip_scaled = reciprocal * (1.0 / math.sqrt(total_cells * CAP * K))
    combined = atom_features.astype(jnp.float32) + short_scaled + recip_scaled.reshape(total_cells, CAP, H)
    return (live_mask[:, :, None] * combined).astype(jnp.bfloat16)
```

```python
import functools
import math

import jax
import jax.numpy as jnp
from jax import lax
from jax.experimental import pallas as pl
from jax.experimental.pallas import tpu as pltpu
from jax.sharding import PartitionSpec as P

GRID = 3
CUTOFF = 1.0
BF16 = jnp.bfloat16
F32 = jnp.float32
COORD_ROWS = 16
LANES = 128
SINE = (4.44287959, -7.30781805, 3.59778873, -0.791238217)
COSINE = (1.4142135, -6.97885099, 5.73946117, -1.88356299, 0.310698193)
HALF_COSINE = (0.999999953, -1.23369821, 0.253650745, -0.0208106275, 0.000858190619)
PARAMS = pltpu.CompilerParams(vmem_limit_bytes=40 * 1024 * 1024)


def horner(coefficients, value):
    total = coefficients[-1]
    for coefficient in coefficients[-2::-1]:
        total = total * value + coefficient
    return total


def turn_cos_sin(scaled, scale):
    turns = scaled * scale
    rest = turns - jnp.round(turns)
    square = rest * rest
    half_sine = horner(SINE, square) * rest
    half_cosine = horner(COSINE, square)
    return (1.0 - half_sine * half_sine, half_sine * half_cosine)


def pad_up(value, unit):
    return -(-value // unit) * unit


def tails_side_by_side(rows_of, width, tail):
    lane = lax.broadcasted_iota(jnp.int32, (COORD_ROWS, width), 1)
    total = jnp.zeros((COORD_ROWS, width), F32)
    for l, rows in enumerate(rows_of):
        total = jnp.where((lane >= l * tail) & (lane < (l + 1) * tail), rows[:, :width], total)
    return total


def structure_kernel(chunk_count, atoms, scale, first, last, *refs):
    chunks = refs[:chunk_count]
    refs = refs[chunk_count:]
    main_ref, tail_ref = refs[:2]
    refs = refs[2:]
    if not first:
        sum_ref, refs = refs[0], refs[1:]
    if last:
        mine_ref, send_ref, refs = refs[0], refs[1], refs[2:]
    else:
        out_ref, refs = refs[0], refs[1:]
    phase_ref, table_ref, stack_ref = refs
    waves = main_ref.shape[0]
    half = waves // 2
    width = chunks[0].shape[1]
    tail = atoms - width
    depth = stack_ref.shape[0]
    tail_width = depth - chunk_count * width
    step = 32

    def fill(first_lane, lanes):
        def body(index, carry):
            row = pl.multiple_of(index * step, step)
            cosine, sine = turn_cos_sin(phase_ref[pl.ds(row, step), 0:lanes], scale)
            place = row + jnp.where(row >= half, half, 0)
            place = pl.multiple_of(place, step)
            table_ref[pl.ds(place, step), first_lane : first_lane + lanes] = cosine.astype(BF16)
            table_ref[pl.ds(place + half, step), first_lane : first_lane + lanes] = sine.astype(BF16)
            return carry

        lax.fori_loop(0, waves // step, body, 0, unroll=2)

    for l, chunk in enumerate(chunks):
        stack_ref[l * width : (l + 1) * width, :] = chunk[0:width, :]
        at = chunk_count * width + l * tail
        stack_ref[at : at + tail, :] = chunk[width:atoms, :]
    used = chunk_count * width + chunk_count * tail
    if used < depth:
        stack_ref[used:depth, :] = jnp.zeros((depth - used, width), BF16)
    for l, chunk in enumerate(chunks):
        phase_ref[...] = jnp.dot(
            main_ref[...], chunk[atoms : atoms + COORD_ROWS, :], preferred_element_type=F32
        )
        fill(l * width, width)
    rows = tails_side_by_side(
        [chunk[atoms : atoms + COORD_ROWS, :].astype(F32) for chunk in chunks], tail_width, tail
    )
    phase_ref[:, 0:tail_width] = jnp.dot(
        tail_ref[...], rows.astype(BF16), preferred_element_type=F32
    )
    fill(chunk_count * width, tail_width)
    total = jnp.dot(table_ref[...], stack_ref[...], preferred_element_type=F32)
    if not first:
        total = total + sum_ref[...]
    if last:
        mine_ref[...] = total[0:waves]
        send_ref[...] = total[waves:].astype(BF16)
    else:
        out_ref[...] = total


def add_structure(chunks, main_waves, tail_waves, running, atoms, scale, last):
    count = len(chunks)
    width = chunks[0].shape[1]
    waves = main_waves.shape[0]
    tail_width = pad_up(count * (atoms - width), LANES)
    depth = count * width + tail_width
    if last:
        shapes = (
            jax.ShapeDtypeStruct((waves, width), F32),
            jax.ShapeDtypeStruct((waves, width), BF16),
        )
    else:
        shapes = jax.ShapeDtypeStruct((2 * waves, width), F32)
    more = () if running is None else (running,)
    return pl.pallas_call(
        functools.partial(structure_kernel, count, atoms, scale, running is None, last),
        out_shape=shapes,
        scratch_shapes=[
            pltpu.VMEM((waves, width), F32),
            pltpu.VMEM((2 * waves, depth), BF16),
            pltpu.VMEM((depth, width), BF16),
        ],
        compiler_params=PARAMS,
        cost_estimate=pl.CostEstimate(
            flops=60 * 2 * waves * depth * width // 10,
            bytes_accessed=8 * waves * width,
            transcendentals=0,
        ),
        name="structure",
    )(*chunks, main_waves, tail_waves, *more)


def own_table_kernel(scale, own_ref, waves_ref, table_ref, phase_ref):
    waves = waves_ref.shape[1]
    half = waves // 2
    atoms = own_ref.shape[0]
    phase_ref[...] = jnp.dot(own_ref[...], waves_ref[...], preferred_element_type=F32)
    step = 16

    def body(index, carry):
        row = pl.multiple_of(index * step, step)
        for block in range(2):
            cosine, sine = turn_cos_sin(
                phase_ref[pl.ds(row, step), block * half : (block + 1) * half], scale
            )
            at = block * waves
            table_ref[pl.ds(row, step), at : at + half] = cosine.astype(BF16)
            table_ref[pl.ds(row, step), at + half : at + waves] = sine.astype(BF16)
        return carry

    lax.fori_loop(0, atoms // step, body, 0)


def own_table(own_cols, main_waves_t, scale):
    atoms, waves = own_cols.shape[0], main_waves_t.shape[1]
    return pl.pallas_call(
        functools.partial(own_table_kernel, scale),
        out_shape=jax.ShapeDtypeStruct((atoms, 2 * waves), BF16),
        scratch_shapes=[pltpu.VMEM((atoms, waves), F32)],
        compiler_params=PARAMS,
        cost_estimate=pl.CostEstimate(
            flops=1200 * atoms * waves, bytes_accessed=4 * atoms * waves, transcendentals=0
        ),
        name="own_table",
    )(own_cols, main_waves_t)


def short_kernel(
    cells, slots, basis_count, side_ref, own_ref, side_chunk_ref, far_ref, cols_ref, radial_ref,
    out_ref, near_ref, weight_ref, mixed_ref,
):
    atoms = cells * slots
    width = own_ref.shape[1]
    tail = atoms - width
    chunks = (own_ref, side_chunk_ref, far_ref)
    near = near_ref.shape[0]
    tail_width = near - 3 * width
    side = side_ref[0].astype(F32)
    shifts = (0.0, side, -side)
    mains, tails = [], []
    tail_lane = lax.broadcasted_iota(jnp.int32, (1, tail_width), 1)
    shift_row = jnp.zeros((1, tail_width), F32)
    for l, chunk in enumerate(chunks):
        near_ref[l * width : (l + 1) * width, :] = chunk[0:width, :]
        at = 3 * width + l * tail
        near_ref[at : at + tail, :] = chunk[width:atoms, :]
        rows = chunk[atoms : atoms + COORD_ROWS, :].astype(F32)
        mains.append(
            (rows[0:1], rows[1:2], rows[3:4], rows[4:5], rows[5:6] + shifts[l])
        )
        tails.append(rows)
        here = (tail_lane >= l * tail) & (tail_lane < (l + 1) * tail)
        shift_row = jnp.where(here, shifts[l], shift_row)
    used = 3 * (width + tail)
    if used < near:
        near_ref[used:near, :] = jnp.zeros((near - used, width), BF16)
    joined = tails_side_by_side(tails, tail_width, tail)
    mains.append(
        (joined[8:9], joined[9:10], joined[11:12], joined[12:13], joined[13:14] + shift_row)
    )
    cell_x, cell_y, off_x, off_y, off_z = (
        jnp.concatenate([part[k] for part in mains], axis=1) for k in range(5)
    )
    lane = lax.broadcasted_iota(jnp.int32, (1, near), 1)
    own_index = jnp.where(
        lane < width,
        lane,
        jnp.where((lane >= 3 * width) & (lane < 3 * width + tail), lane - 2 * width, near),
    )

    def wrapped(delta):
        return jnp.where(
            delta >= GRID - 1.0, delta - GRID, jnp.where(delta < -1.0, delta + GRID, delta)
        )

    step = 16
    sharp = basis_count / CUTOFF
    for cell in range(cells):
        row_x = wrapped(cell_x - float(cell // GRID)) + off_x
        row_y = wrapped(cell_y - float(cell % GRID)) + off_y
        for row in range(cell * slots, (cell + 1) * slots, step):
            own = cols_ref[row : row + step, :].astype(F32)
            delta_x = row_x - own[:, 3:4]
            delta_y = row_y - own[:, 4:5]
            delta_z = off_z - own[:, 5:6]
            square = delta_x * delta_x + delta_y * delta_y + delta_z * delta_z
            radius = jnp.sqrt(square)
            root = horner(HALF_COSINE, square * (1.0 / (CUTOFF * CUTOFF)))
            own_row = row + lax.broadcasted_iota(jnp.int32, (step, 1), 0)
            counted = (radius < CUTOFF) & (own_index != own_row)
            smooth = jnp.where(counted, root * root, 0.0)
            for basis in range(basis_count):
                scaled = (radius - (basis + 0.5) * CUTOFF / basis_count) * sharp
                weight_ref[basis * atoms + row : basis * atoms + row + step, :] = (
                    jnp.exp(-(scaled * scaled)) * smooth
                ).astype(BF16)
    for basis in range(basis_count):
        mixed_ref[:, basis * width : (basis + 1) * width] = jnp.dot(
            weight_ref[basis * atoms : (basis + 1) * atoms, :],
            near_ref[...],
            preferred_element_type=F32,
        ).astype(BF16)
    out_ref[...] = jnp.dot(mixed_ref[...], radial_ref[...], preferred_element_type=F32)


def short_range(side, own, side_chunk, far, own_cols, radial_flat, cells, slots, basis_count):
    atoms = cells * slots
    width = own.shape[1]
    near = 3 * width + pad_up(3 * (atoms - width), LANES)
    vmem = pl.BlockSpec(memory_space=pltpu.VMEM)
    return pl.pallas_call(
        functools.partial(short_kernel, cells, slots, basis_count),
        out_shape=jax.ShapeDtypeStruct((atoms, width), F32),
        in_specs=[pl.BlockSpec(memory_space=pltpu.SMEM)] + [vmem] * 5,
        out_specs=vmem,
        scratch_shapes=[
            pltpu.VMEM((near, width), BF16),
            pltpu.VMEM((basis_count * atoms, near), BF16),
            pltpu.VMEM((atoms, basis_count * width), BF16),
        ],
        compiler_params=PARAMS,
        cost_estimate=pl.CostEstimate(
            flops=10 * basis_count * atoms * near * width, bytes_accessed=4 * near * width,
            transcendentals=0,
        ),
        name="short_range",
    )(side, own, side_chunk, far, own_cols, radial_flat)


def filter_kernel(mine_ref, other_ref, charge_ref, gain_ref, out_ref):
    half = gain_ref.shape[0]
    total = mine_ref[...] + other_ref[...].astype(F32)
    structure = jnp.dot(total.astype(BF16), charge_ref[...], preferred_element_type=F32)
    gain = gain_ref[...]
    out_ref[0:half] = (structure[0:half] * gain).astype(BF16)
    out_ref[half:] = (structure[half:] * gain).astype(BF16)


def filter_half(mine, other, charge_weight, gain):
    return pl.pallas_call(
        filter_kernel,
        out_shape=jax.ShapeDtypeStruct(mine.shape, BF16),
        compiler_params=PARAMS,
        name="filter",
    )(mine, other, charge_weight, gain)


def inverse_kernel(scale, table_ref, factor_ref, base_ref, out_ref):
    out_ref[...] = base_ref[...] + scale * jnp.dot(
        table_ref[...], factor_ref[...], preferred_element_type=F32
    )


def finish_kernel(scale, slots, counts_ref, table_ref, factor_ref, base_ref, out_ref):
    total = base_ref[...] + scale * jnp.dot(
        table_ref[...], factor_ref[...], preferred_element_type=F32
    )
    slot = lax.broadcasted_iota(jnp.int32, (slots, total.shape[1]), 0)
    for cell in range(total.shape[0] // slots):
        rows = total[cell * slots : (cell + 1) * slots]
        out_ref[cell] = jnp.where(slot < counts_ref[cell], rows, 0.0).astype(BF16)


def local(atom_features, offsets, counts, radial_weight, charge_weight, wave_filter, wavevectors):
    cells, slots, width = atom_features.shape
    atoms = cells * slots
    basis_count = radial_weight.shape[0]
    wave_count = wavevectors.shape[1]
    size = lax.axis_size("space")
    layer = lax.axis_index("space")
    cores = 2 if size % 2 == 0 else 1
    near_y = 2 if (size // cores) % 2 == 0 else 1
    deep = size // (cores * near_y)
    core = layer % cores
    half = wave_count // 2

    slot_ids = jnp.arange(slots, dtype=jnp.int32)
    live = slot_ids[None, :] < counts[:, None]
    masked = jnp.where(live[:, :, None], atom_features, jnp.zeros((), BF16)).reshape(atoms, width)
    cell_ids = jnp.arange(cells, dtype=jnp.int32)
    cell_of = jnp.repeat(cell_ids, slots)
    flat_offsets = jnp.transpose(offsets, (1, 0, 2)).reshape(3, atoms)
    places = jnp.concatenate(
        [
            jnp.stack(
                [cell_of // GRID, cell_of % GRID, jnp.broadcast_to(layer, (atoms,))]
            ).astype(BF16),
            flat_offsets,
            jnp.zeros((2, atoms), BF16),
        ],
        axis=0,
    )
    tail = atoms - width
    coords = jnp.concatenate(
        [places[:, :width], jnp.tile(places[:, width:], (1, width // tail))], axis=0
    )
    payload = jnp.concatenate([masked, coords], axis=0)

    def swap(value, mask):
        return lax.ppermute(value, "space", [(i, i ^ mask) for i in range(size)])

    stride = cores * near_y
    along = {k: swap(payload, k * stride) for k in range(deep - 1, 0, -1)}
    beside = swap(payload, cores)
    pair = swap(payload, 1)
    across = {k: swap(along[k], cores) for k in sorted(along)}

    own_half = lax.dynamic_slice_in_dim(wavevectors, core * half, half, 1)
    other_half = lax.dynamic_slice_in_dim(wavevectors, (1 - core) * half, half, 1)
    waves = jnp.concatenate([own_half, other_half], axis=1)
    steps = jnp.array([[size], [size], [GRID]], jnp.int32)
    one = (waves * steps).astype(BF16)
    blank = jnp.zeros((2, wave_count), BF16)
    rows_main = jnp.concatenate([one, one, blank, jnp.zeros((8, wave_count), BF16)], axis=0)
    rows_tail = jnp.concatenate([jnp.zeros((8, wave_count), BF16), one, one, blank], axis=0)
    main_waves, tail_waves = rows_main.T, rows_tail.T
    scale = 1.0 / (GRID * size)
    own_cols = jnp.concatenate([places, jnp.zeros((8, atoms), BF16)], axis=0).T

    two_pi = 2.0 * math.pi
    wave_float = own_half.astype(F32)
    along_x = two_pi * wave_float[0] / GRID
    along_y = two_pi * wave_float[1] / GRID
    along_z = two_pi * wave_float[2] / size
    magnitude = jnp.sqrt(along_x * along_x + along_y * along_y + along_z * along_z)
    gain = jnp.zeros((half, width), F32)
    for b in range(wave_filter.shape[0]):
        offset_k = (magnitude - 3.0 * b) / 3.0
        gain = gain + jnp.exp(-(offset_k * offset_k))[:, None] * wave_filter[b][None, :]

    table = own_table(own_cols, rows_main, scale)

    z = layer // stride
    y = (layer // cores) % near_y
    step_z = jnp.where(core == 0, 1, deep - 1)
    wanted = z ^ ((z + step_z) % deep)
    crossing = beside
    for k in across:
        if k & (k + 1) == 0:
            take = (wanted == k) & (y == jnp.where(core == 0, near_y - 1, 0))
            crossing = jnp.where(take, across[k], crossing)
    far = swap(crossing, 1)
    side = jnp.where(core == 0, 1, -1).astype(jnp.int32).reshape(1)
    short = short_range(
        side, payload, pair, far, own_cols, radial_weight.reshape(basis_count * width, width),
        cells, slots, basis_count,
    )

    early = [payload, beside] + [along[k] for k in along]
    late = [across[k] for k in across]
    groups = [early[i : i + 4] for i in range(0, len(early), 4)]
    groups += [late[i : i + 4] for i in range(0, len(late), 4)]
    running = None
    for index, group in enumerate(groups):
        running = add_structure(
            group, main_waves, tail_waves, running, atoms, scale, index == len(groups) - 1
        )
    mine, send = running
    factors = filter_half(mine, swap(send, 1), charge_weight, gain)
    other_factors = swap(factors, 1)

    base = atom_features.reshape(atoms, width).astype(F32) + short * (1.0 / math.sqrt(slots))
    recip_scale = 1.0 / math.sqrt(atoms * size * wave_count)
    vmem = pl.BlockSpec(memory_space=pltpu.VMEM)
    base = pl.pallas_call(
        functools.partial(inverse_kernel, recip_scale),
        grid=(1,),
        in_specs=[
            pl.BlockSpec((atoms, wave_count), lambda i: (0, 0)),
            pl.BlockSpec((wave_count, width), lambda i: (0, 0)),
            pl.BlockSpec((atoms, width), lambda i: (0, 0)),
        ],
        out_specs=pl.BlockSpec((atoms, width), lambda i: (0, 0)),
        out_shape=jax.ShapeDtypeStruct((atoms, width), F32),
        compiler_params=PARAMS,
        name="inverse",
    )(table, factors, base)
    return pl.pallas_call(
        functools.partial(finish_kernel, recip_scale, slots),
        grid=(1,),
        in_specs=[
            pl.BlockSpec(memory_space=pltpu.SMEM),
            pl.BlockSpec((atoms, wave_count), lambda i: (0, 1)),
            pl.BlockSpec((wave_count, width), lambda i: (0, 0)),
            pl.BlockSpec((atoms, width), lambda i: (0, 0)),
        ],
        out_specs=pl.BlockSpec((cells, slots, width), lambda i: (0, 0, 0)),
        out_shape=jax.ShapeDtypeStruct((cells, slots, width), BF16),
        compiler_params=PARAMS,
        name="finish",
    )(counts, table, other_factors, base)


def solution(mesh):
    in_specs = (
        P(("groups", "space"), None, None),
        P(("groups", "space"), None, None),
        P(("groups", "space")),
        P(),
        P(),
        P(),
        P(),
    )
    out_specs = P(("groups", "space"), None, None)
    return jax.shard_map(local, mesh=mesh, in_specs=in_specs, out_specs=out_specs, check_vma=False)
```

```python
import functools
import math

import jax
import jax.numpy as jnp
from jax import lax
from jax.experimental import pallas as pl
from jax.experimental.pallas import tpu as pltpu
from jax.sharding import PartitionSpec as P

GRID = 3
CUTOFF = 1.0
BF16 = jnp.bfloat16
F32 = jnp.float32
COORD_ROWS = 16
LANES = 128
SINE = (4.44287959, -7.30781805, 3.59778873, -0.791238217)
COSINE = (1.4142135, -6.97885099, 5.73946117, -1.88356299, 0.310698193)
HALF_COSINE = (0.999999953, -1.23369821, 0.253650745, -0.0208106275, 0.000858190619)
PARAMS = pltpu.CompilerParams(vmem_limit_bytes=32 * 1024 * 1024)
WIDE = pltpu.CompilerParams(vmem_limit_bytes=62 * 1024 * 1024)


def horner(coefficients, value):
    total = coefficients[-1]
    for coefficient in coefficients[-2::-1]:
        total = total * value + coefficient
    return total


def turn_cos_sin(scaled, scale):
    turns = scaled * scale
    rest = turns - jnp.round(turns)
    square = rest * rest
    half_sine = horner(SINE, square) * rest
    half_cosine = horner(COSINE, square)
    return (1.0 - half_sine * half_sine, half_sine * half_cosine)


def cost(flops):
    return pl.CostEstimate(flops=flops, bytes_accessed=flops // 1000, transcendentals=0)


def in_hbm(value):
    return pltpu.with_memory_space_constraint(value, pltpu.HBM)


def pad_up(value, unit):
    return -(-value // unit) * unit


def tails_side_by_side(rows_of, width, tail):
    lane = lax.broadcasted_iota(jnp.int32, (COORD_ROWS, width), 1)
    total = jnp.zeros((COORD_ROWS, width), F32)
    for l, rows in enumerate(rows_of):
        total = jnp.where((lane >= l * tail) & (lane < (l + 1) * tail), rows[:, :width], total)
    return total


def prepare_kernel(
    layer_ref, counts_any, features_any, offsets_any, payload_ref, cols_ref,
    counts_ref, features_ref, offsets_ref, rows_ref, sems,
):
    copies = [
        pltpu.make_async_copy(source, target, sems.at[i])
        for i, (source, target) in enumerate(
            ((features_any, features_ref), (offsets_any, offsets_ref), (counts_any, counts_ref))
        )
    ]
    for copy in copies:
        copy.start()
    cells, slots, width = features_ref.shape
    atoms = cells * slots
    tail = atoms - width
    slot = lax.broadcasted_iota(jnp.int32, (slots, width), 0)
    lane = lax.broadcasted_iota(jnp.int32, (1, width), 1)
    main_cells = width // slots
    for copy in copies[1:]:
        copy.wait()
    within = [offsets_ref[cell].astype(F32) for cell in range(cells)]
    for first, parts in (
        (0, list(range(main_cells))),
        (8, list(range(main_cells, cells)) * (width // tail)),
    ):
        along_x = jnp.zeros((1, width), F32)
        along_y = jnp.zeros((1, width), F32)
        lives = jnp.zeros((1, width), jnp.int32)
        for place, cell in enumerate(parts):
            here = (lane >= place * slots) & (lane < (place + 1) * slots)
            along_x = jnp.where(here, float(cell // GRID), along_x)
            along_y = jnp.where(here, float(cell % GRID), along_y)
            lives = jnp.where(here, counts_ref[cell] + place * slots, lives)
        rows_ref[first : first + 1, :] = along_x
        rows_ref[first + 1 : first + 2, :] = along_y
        rows_ref[first + 2 : first + 3, :] = jnp.full((1, width), layer_ref[0].astype(F32))
        rows_ref[first + 3 : first + 6, :] = jnp.concatenate([within[c] for c in parts], axis=1)
        rows_ref[first + 6 : first + 7, :] = jnp.where(lane < lives, 1.0, 0.0)
        rows_ref[first + 7 : first + 8, :] = jnp.zeros((1, width), F32)
    rows = rows_ref[...]
    payload_ref[atoms : atoms + COORD_ROWS, :] = rows.astype(BF16)
    cols_ref[0:width, :] = rows.T
    cols_ref[width:atoms, 0:8] = rows[8:16, 0:LANES].T[0:tail]
    cols_ref[width:atoms, 8:16] = jnp.zeros((tail, 8), F32)
    copies[0].wait()
    for cell in range(cells):
        rows = features_ref[cell].astype(F32)
        payload_ref[cell * slots : (cell + 1) * slots, :] = jnp.where(
            slot < counts_ref[cell], rows, 0.0
        ).astype(BF16)


def prepare(layer, counts, atom_features, offsets):
    cells, slots, width = atom_features.shape
    atoms = cells * slots
    smem = pl.BlockSpec(memory_space=pltpu.SMEM)
    vmem = pl.BlockSpec(memory_space=pltpu.VMEM)
    anywhere = pl.BlockSpec(memory_space=pltpu.HBM)
    return pl.pallas_call(
        prepare_kernel,
        out_shape=(
            jax.ShapeDtypeStruct((atoms + COORD_ROWS, width), BF16),
            jax.ShapeDtypeStruct((atoms, COORD_ROWS), F32),
        ),
        in_specs=[smem, anywhere, anywhere, anywhere],
        out_specs=(vmem, vmem),
        scratch_shapes=[
            pltpu.SMEM(counts.shape, jnp.int32),
            pltpu.VMEM(atom_features.shape, BF16),
            pltpu.VMEM(offsets.shape, BF16),
            pltpu.VMEM((COORD_ROWS, width), F32),
            pltpu.SemaphoreType.DMA((3,)),
        ],
        compiler_params=PARAMS,
        name="prepare",
    )(layer, *map(in_hbm, (counts, atom_features, offsets)))


def wave_kernel(
    size, core_ref, waves_any, filter_any, payload_ref, rows_ref, main_ref, tail_ref, gain_ref, passed_ref,
    waves_ref, filter_ref, all_ref, sems,
):
    copies = (
        pltpu.make_async_copy(waves_any, waves_ref, sems.at[0]),
        pltpu.make_async_copy(filter_any, filter_ref, sems.at[1]),
    )
    for copy in copies:
        copy.start()
    passed_ref[...] = payload_ref[...]
    for copy in copies:
        copy.wait()
    wave_count = waves_ref.shape[1]
    half = wave_count // 2
    basis_count, width = filter_ref.shape
    core = core_ref[0]
    all_ref[...] = jnp.zeros(all_ref.shape, F32)
    for place in range(2):
        start = pl.multiple_of((core if place == 0 else 1 - core) * half, LANES)
        taken = waves_ref[:, pl.ds(start, half)].astype(F32)
        at = slice(place * half, (place + 1) * half)
        for first in (0, 3):
            all_ref[first : first + 2, at] = taken[0:2] * float(size)
            all_ref[first + 2 : first + 3, at] = taken[2:3] * float(GRID)
    rows = all_ref[...]
    rows_ref[...] = rows.astype(BF16)
    columns = rows.T
    main_ref[...] = columns.astype(BF16)
    tail_ref[...] = jnp.concatenate([rows[8:16], rows[0:8]], axis=0).T.astype(BF16)
    own = columns[0:half]
    per_step = 2.0 * math.pi / (GRID * size)
    along_x, along_y, along_z = own[:, 0:1] * per_step, own[:, 1:2] * per_step, own[:, 2:3] * per_step
    magnitude = jnp.sqrt(along_x * along_x + along_y * along_y + along_z * along_z)
    gain = jnp.zeros((half, width), F32)
    for b in range(basis_count):
        offset_k = (magnitude - 3.0 * b) * (1.0 / 3.0)
        gain = gain + jnp.exp(-(offset_k * offset_k)) * filter_ref[b : b + 1, :]
    gain_ref[...] = gain


def wave_tables(core, wavevectors, wave_filter, size, payload):
    wave_count, width = wavevectors.shape[1], wave_filter.shape[1]
    vmem = pl.BlockSpec(memory_space=pltpu.VMEM)
    return pl.pallas_call(
        functools.partial(wave_kernel, size),
        out_shape=(
            jax.ShapeDtypeStruct((COORD_ROWS, wave_count), BF16),
            jax.ShapeDtypeStruct((wave_count, COORD_ROWS), BF16),
            jax.ShapeDtypeStruct((wave_count, COORD_ROWS), BF16),
            jax.ShapeDtypeStruct((wave_count // 2, width), F32),
            jax.ShapeDtypeStruct(payload.shape, payload.dtype),
        ),
        in_specs=[pl.BlockSpec(memory_space=pltpu.SMEM)] + [pl.BlockSpec(memory_space=pltpu.HBM)] * 2
        + [vmem],
        out_specs=(vmem,) * 5,
        scratch_shapes=[
            pltpu.VMEM(wavevectors.shape, jnp.int32),
            pltpu.VMEM(wave_filter.shape, F32),
            pltpu.VMEM((COORD_ROWS, wave_count), F32),
            pltpu.SemaphoreType.DMA((2,)),
        ],
        compiler_params=PARAMS,
        name="waves",
    )(core, in_hbm(wavevectors), in_hbm(wave_filter), payload)


def structure_kernel(chunk_count, atoms, scale, parts, *refs):
    chunks, refs = refs[:chunk_count], refs[chunk_count:]
    main_ref, tail_ref, _, refs = refs[0], refs[1], refs[2], refs[3:]
    count = len(parts)
    sums, outs, refs = refs[:count], refs[count : 2 * count], refs[2 * count :]
    phases, tables, stack_ref = refs[:count], refs[count : 2 * count], refs[2 * count]
    half = main_ref.shape[0] // 2
    width = chunks[0].shape[1]
    tail = atoms - width
    depth = stack_ref.shape[0]
    split = chunk_count * width
    step = 32
    for l, chunk in enumerate(chunks):
        stack_ref[l * width : (l + 1) * width, :] = chunk[0:width, :]
        at = split + l * tail
        stack_ref[at : at + tail, :] = chunk[width:atoms, :]
    used = chunk_count * atoms
    if used < depth:
        stack_ref[used:depth, :] = jnp.zeros((depth - used, width), BF16)
    rows = tails_side_by_side(
        [chunk[atoms : atoms + COORD_ROWS, :].astype(F32) for chunk in chunks], depth - split, tail
    )
    for part, sum_ref, out_ref, phase_ref, table_ref in zip(parts, sums, outs, phases, tables):
        waves = slice(part * half, (part + 1) * half)
        for l, chunk in enumerate(chunks):
            phase_ref[:, l * width : (l + 1) * width] = jnp.dot(
                main_ref[waves], chunk[atoms : atoms + COORD_ROWS, :], preferred_element_type=F32
            )
        phase_ref[:, split:depth] = jnp.dot(
            tail_ref[waves], rows.astype(BF16), preferred_element_type=F32
        )
        for first_lane in range(0, depth, width):
            here = slice(first_lane, min(first_lane + width, depth))
            for row in range(0, half, step):
                cosine, sine = turn_cos_sin(phase_ref[row : row + step, here], scale)
                table_ref[row : row + step, here] = cosine.astype(BF16)
                table_ref[half + row : half + row + step, here] = sine.astype(BF16)
        total = jnp.dot(table_ref[...], stack_ref[...], preferred_element_type=F32)
        out_ref[...] = (total + sum_ref[...]).astype(out_ref.dtype)


def add_structure(chunks, parts, main_waves, tail_waves, token, sums, atoms, scale, kept_as=F32):
    count = len(chunks)
    width = chunks[0].shape[1]
    half = main_waves.shape[0] // 2
    depth = count * width + pad_up(count * (atoms - width), LANES)
    vmem = pl.BlockSpec(memory_space=pltpu.VMEM)
    return pl.pallas_call(
        functools.partial(structure_kernel, count, atoms, scale, parts),
        in_specs=[vmem] * (count + 2) + [pl.BlockSpec(memory_space=pl.ANY)] + [vmem] * len(parts),
        out_specs=[vmem] * len(parts),
        out_shape=[jax.ShapeDtypeStruct((2 * half, width), kept_as)] * len(parts),
        scratch_shapes=[pltpu.VMEM((half, depth), F32)] * len(parts)
        + [pltpu.VMEM((2 * half, depth), BF16)] * len(parts)
        + [pltpu.VMEM((depth, width), BF16)],
        compiler_params=PARAMS,
        cost_estimate=cost(12 * half * len(parts) * depth * width),
        name="structure",
    )(*chunks, main_waves, tail_waves, token, *sums)


def own_kernel(scale, cols_ref, waves_ref, payload_ref, table_ref, mine_ref, other_ref, phase_ref):
    waves = waves_ref.shape[1]
    half = waves // 2
    atoms = cols_ref.shape[0]
    phase_ref[...] = jnp.dot(
        cols_ref[...].astype(BF16), waves_ref[...], preferred_element_type=F32
    )
    step = 16
    for part, out_ref in enumerate((mine_ref, other_ref)):
        at = part * waves
        for row in range(0, atoms, step):
            cosine, sine = turn_cos_sin(
                phase_ref[row : row + step, part * half : (part + 1) * half], scale
            )
            table_ref[row : row + step, at : at + half] = cosine.astype(BF16)
            table_ref[row : row + step, at + half : at + waves] = sine.astype(BF16)
        out_ref[...] = lax.dot_general(
            table_ref[:, at : at + waves],
            payload_ref[0:atoms, :],
            (((0,), (0,)), ((), ())),
            preferred_element_type=F32,
        )


def own_layer(own_cols, wave_rows, payload, scale):
    atoms, waves = own_cols.shape[0], wave_rows.shape[1]
    width = payload.shape[1]
    return pl.pallas_call(
        functools.partial(own_kernel, scale),
        out_shape=(
            jax.ShapeDtypeStruct((atoms, 2 * waves), BF16),
            jax.ShapeDtypeStruct((waves, width), F32),
            jax.ShapeDtypeStruct((waves, width), F32),
        ),
        scratch_shapes=[pltpu.VMEM((atoms, waves), F32)],
        compiler_params=PARAMS,
        cost_estimate=cost(4 * atoms * waves * width),
        name="own_layer",
    )(own_cols, wave_rows, payload)


def short_kernel(cells, slots, basis_count, signs, holds_own, last, scale, *refs):
    count = len(signs)
    side_ref, refs = refs[0], refs[1:]
    chunks, refs = refs[:count], refs[count:]
    cols_ref, radial_ref, refs = refs[0], refs[1], refs[2:]
    if last:
        before_ref, features_ref, refs = refs[0], refs[1], refs[2:]
    out_ref, near_ref, weight_ref, mixed_ref = refs
    atoms = cells * slots
    width = chunks[0].shape[1]
    tail = atoms - width
    near = near_ref.shape[0]
    tail_width = near - count * width
    side = side_ref[0].astype(F32)
    shifts = [sign * side for sign in signs]
    mains, tails = [], []
    tail_lane = lax.broadcasted_iota(jnp.int32, (1, tail_width), 1)
    shift_row = jnp.zeros((1, tail_width), F32)
    for l, chunk in enumerate(chunks):
        near_ref[l * width : (l + 1) * width, :] = chunk[0:width, :]
        at = count * width + l * tail
        near_ref[at : at + tail, :] = chunk[width:atoms, :]
        rows = chunk[atoms : atoms + COORD_ROWS, :].astype(F32)
        mains.append((rows[0:1], rows[1:2], rows[3:4], rows[4:5], rows[5:6] + shifts[l]))
        tails.append(rows)
        here = (tail_lane >= l * tail) & (tail_lane < (l + 1) * tail)
        shift_row = jnp.where(here, shifts[l], shift_row)
    used = count * (width + tail)
    if used < near:
        near_ref[used:near, :] = jnp.zeros((near - used, width), BF16)
    joined = tails_side_by_side(tails, tail_width, tail)
    mains.append(
        (joined[8:9], joined[9:10], joined[11:12], joined[12:13], joined[13:14] + shift_row)
    )
    cell_x, cell_y, off_x, off_y, off_z = (
        jnp.concatenate([part[k] for part in mains], axis=1) for k in range(5)
    )
    lane = lax.broadcasted_iota(jnp.int32, (1, near), 1)
    own_index = jnp.where(
        lane < width,
        lane,
        jnp.where(
            (lane >= count * width) & (lane < count * width + tail),
            lane - (count - 1) * width,
            near,
        ),
    )

    def wrapped(delta):
        return jnp.where(
            delta >= GRID - 1.0, delta - GRID, jnp.where(delta < -1.0, delta + GRID, delta)
        )

    step = 16
    sharp = basis_count / CUTOFF
    for cell in range(cells):
        row_x = wrapped(cell_x - float(cell // GRID)) + off_x
        row_y = wrapped(cell_y - float(cell % GRID)) + off_y
        for row in range(cell * slots, (cell + 1) * slots, step):
            own = cols_ref[row : row + step, :]
            delta_x = row_x - own[:, 3:4]
            delta_y = row_y - own[:, 4:5]
            delta_z = off_z - own[:, 5:6]
            square = delta_x * delta_x + delta_y * delta_y + delta_z * delta_z
            root = horner(HALF_COSINE, square * (1.0 / (CUTOFF * CUTOFF)))
            counted = square < CUTOFF * CUTOFF
            if holds_own:
                own_row = row + lax.broadcasted_iota(jnp.int32, (step, 1), 0)
                counted = counted & (own_index != own_row)
            smooth = jnp.where(counted, root * root, 0.0)
            scaled = jnp.sqrt(square) * sharp - 0.5
            weight = jnp.exp(-(scaled * scaled)) * smooth
            growth = jnp.exp(2.0 * scaled)
            for basis in range(basis_count):
                if basis:
                    weight = weight * (growth * math.exp(1.0 - 2.0 * basis))
                weight_ref[basis * atoms + row : basis * atoms + row + step, :] = weight.astype(BF16)
    for basis in range(basis_count):
        mixed_ref[:, basis * width : (basis + 1) * width] = jnp.dot(
            weight_ref[basis * atoms : (basis + 1) * atoms, :],
            near_ref[...],
            preferred_element_type=F32,
        ).astype(BF16)
    total = jnp.dot(mixed_ref[...], radial_ref[...], preferred_element_type=F32)
    if last:
        total = (total + before_ref[...]) * scale + features_ref[0:atoms, :].astype(F32)
    out_ref[...] = total


def short_range(side, chunks, signs, own_cols, radial_flat, slots, basis_count, before=None):
    atoms = own_cols.shape[0]
    count = len(chunks)
    width = chunks[0].shape[1]
    near = count * width + pad_up(count * (atoms - width), LANES)
    last = before is not None
    more = before if last else ()
    vmem = pl.BlockSpec(memory_space=pltpu.VMEM)
    scale = 1.0 / math.sqrt(slots)
    return pl.pallas_call(
        functools.partial(
            short_kernel, atoms // slots, slots, basis_count, signs, not last, last, scale
        ),
        out_shape=jax.ShapeDtypeStruct((atoms, width), F32),
        in_specs=[pl.BlockSpec(memory_space=pltpu.SMEM)] + [vmem] * (count + 2 + len(more)),
        out_specs=vmem,
        scratch_shapes=[
            pltpu.VMEM((near, width), BF16),
            pltpu.VMEM((basis_count * atoms, near), BF16),
            pltpu.VMEM((atoms, basis_count * width), BF16),
        ],
        compiler_params=PARAMS,
        cost_estimate=cost(10 * basis_count * atoms * near * width),
        name="short_range",
    )(side, *chunks, own_cols, radial_flat, *more)


def filter_kernel(mine_ref, other_ref, charge_ref, gain_ref, out_ref):
    half = gain_ref.shape[0]
    total = mine_ref[...] + other_ref[...].astype(F32)
    structure = jnp.dot(total.astype(BF16), charge_ref[...], preferred_element_type=F32)
    gain = gain_ref[...]
    out_ref[0:half] = (structure[0:half] * gain).astype(BF16)
    out_ref[half:] = (structure[half:] * gain).astype(BF16)


def filter_half(mine, other, charge_weight, gain):
    return pl.pallas_call(
        filter_kernel,
        out_shape=jax.ShapeDtypeStruct(mine.shape, BF16),
        compiler_params=PARAMS,
        name="filter",
    )(mine, other, charge_weight, gain)


def inverse_kernel(scale, table_ref, factor_ref, base_ref, out_ref):
    out_ref[...] = base_ref[...] + scale * jnp.dot(
        table_ref[...], factor_ref[...], preferred_element_type=F32
    )


def finish_kernel(scale, slots, cols_ref, table_ref, factor_ref, base_ref, out_ref):
    total = base_ref[...] + scale * jnp.dot(
        table_ref[...], factor_ref[...], preferred_element_type=F32
    )
    total = jnp.where(cols_ref[:, 6:7] > 0.5, total, 0.0)
    for cell in range(total.shape[0] // slots):
        out_ref[cell] = total[cell * slots : (cell + 1) * slots].astype(BF16)


def local(atom_features, offsets, counts, radial_weight, charge_weight, wave_filter, wavevectors):
    cells, slots, width = atom_features.shape
    atoms = cells * slots
    basis_count = radial_weight.shape[0]
    wave_count = wavevectors.shape[1]
    size = lax.axis_size("space")
    layer = lax.axis_index("space")
    cores = 2 if size % 2 == 0 else 1
    near_y = 2 if (size // cores) % 2 == 0 else 1
    deep = size // (cores * near_y)
    core = layer % cores
    layer_scalar = layer.astype(jnp.int32).reshape(1)
    core_scalar = core.astype(jnp.int32).reshape(1)
    payload, own_cols = prepare(layer_scalar, counts, atom_features, offsets)

    def swap(value, mask):
        return lax.ppermute(value, "space", [(i, i ^ mask) for i in range(size)])

    rows_main, main_waves, tail_waves, gain, second = wave_tables(
        core_scalar, wavevectors, wave_filter, size, payload
    )
    scale = 1.0 / (GRID * size)
    table, *sums = own_layer(own_cols, rows_main, second, scale)
    side = 1 - 2 * core_scalar
    radial_flat = radial_weight.reshape(basis_count * width, width)

    stride = cores * near_y
    near_keys = [k for k in range(1, deep) if k == 1]
    far_keys = [k for k in range(deep - 1, 2, -1)]
    last_keys = [k for k in range(1, deep) if k == 2]
    along = {k: swap(payload, k * stride) for k in far_keys + last_keys}
    along.update({k: swap(payload, k * stride) for k in near_keys})
    beside = swap(payload, cores)
    pair = swap(payload, 1)

    def structure(chunks, parts, token, sums, kept_as=F32):
        groups = [chunks[i : i + 4] for i in range(0, len(chunks), 4)]
        for index, group in enumerate(groups):
            kind = kept_as if index == len(groups) - 1 else F32
            sums = add_structure(
                group, parts, main_waves, tail_waves, token, sums, atoms, scale, kind
            )
        return sums

    def after(value, token):
        return lax.optimization_barrier((value, token))[0]

    both = (0, 1)
    across = {k: swap(after(along[k], table), cores) for k in near_keys}
    sums = structure([beside] + [along[k] for k in near_keys], both, side, sums)
    first = dict(across)
    for k in far_keys:
        across[k] = swap(after(along[k], (sums[1], first)), cores)
    short = short_range(side, (second, pair), (0.0, 1.0), own_cols, radial_flat, slots, basis_count)
    for k in last_keys:
        across[k] = swap(after(along[k], short), cores)

    z = layer // stride
    y = (layer // cores) % near_y
    step_z = jnp.where(core == 0, 1, deep - 1)
    wanted = z ^ ((z + step_z) % deep)
    crossing = beside
    for k in across:
        if k & (k + 1) == 0:
            take = (wanted == k) & (y == jnp.where(core == 0, near_y - 1, 0))
            crossing = jnp.where(take, across[k], crossing)
    far = swap(crossing, 1)
    sums = structure(
        [along[k] for k in far_keys] + [across[k] for k in near_keys] + [along[k] for k in last_keys]
        + [across[k] for k in far_keys],
        both, short, sums,
    )
    base = short_range(
        side, (far,), (-1.0,), own_cols, radial_flat, slots, basis_count, (short, second)
    )
    final = [across[k] for k in last_keys]
    (send,) = structure(final, (1,), base, sums[1:], BF16)
    (mine,) = structure(final, (0,), send, sums[:1])
    factors = filter_half(mine, swap(send, 1), charge_weight, gain)
    other_factors = swap(factors, 1)

    recip_scale = 1.0 / math.sqrt(atoms * size * wave_count)
    vmem = pl.BlockSpec(memory_space=pltpu.VMEM)
    base = pl.pallas_call(
        functools.partial(inverse_kernel, recip_scale),
        grid=(1,),
        in_specs=[
            pl.BlockSpec((atoms, wave_count), lambda i: (0, 0)),
            pl.BlockSpec((wave_count, width), lambda i: (0, 0)),
            pl.BlockSpec((atoms, width), lambda i: (0, 0)),
        ],
        out_specs=pl.BlockSpec((atoms, width), lambda i: (0, 0)),
        out_shape=jax.ShapeDtypeStruct((atoms, width), F32),
        compiler_params=PARAMS,
        name="inverse",
    )(table, factors, base)
    return pl.pallas_call(
        functools.partial(finish_kernel, recip_scale, slots),
        grid=(1,),
        in_specs=[
            pl.BlockSpec((atoms, COORD_ROWS), lambda i: (0, 0)),
            pl.BlockSpec((atoms, wave_count), lambda i: (0, 1)),
            pl.BlockSpec((wave_count, width), lambda i: (0, 0)),
            pl.BlockSpec((atoms, width), lambda i: (0, 0)),
        ],
        out_specs=pl.BlockSpec((cells, slots, width), lambda i: (0, 0, 0)),
        out_shape=jax.ShapeDtypeStruct((cells, slots, width), BF16),
        compiler_params=PARAMS,
        name="finish",
    )(own_cols, table, other_factors, base)


def solution(mesh):
    in_specs = (
        P(("groups", "space"), None, None),
        P(("groups", "space"), None, None),
        P(("groups", "space")),
        P(),
        P(),
        P(),
        P(),
    )
    out_specs = P(("groups", "space"), None, None)
    return jax.shard_map(local, mesh=mesh, in_specs=in_specs, out_specs=out_specs, check_vma=False)
```

```python
import functools
import math

import jax
import jax.numpy as jnp
from jax import lax
from jax.experimental import pallas as pl
from jax.experimental.pallas import tpu as pltpu
from jax.sharding import PartitionSpec as P

GRID = 3
CUTOFF = 1.0
BF16 = jnp.bfloat16
F32 = jnp.float32
COORD_ROWS = 16
LANES = 128
TERMS = 3
SINE = (4.44287959, -7.30781805, 3.59778873, -0.791238217)
COSINE = (1.41420408, -6.97764206, 5.7152384, -1.72834866)
HALF_COSINE = (0.999999953, -1.23369821, 0.253650745, -0.0208106275, 0.000858190619)
PARAMS = pltpu.CompilerParams(vmem_limit_bytes=32 * 1024 * 1024)
WIDE = pltpu.CompilerParams(vmem_limit_bytes=62 * 1024 * 1024)


def horner(coefficients, value):
    total = coefficients[-1]
    for coefficient in coefficients[-2::-1]:
        total = total * value + coefficient
    return total


def turn_cos_sin(turns):
    rest = turns - jnp.round(turns)
    square = rest * rest
    half_sine = horner(SINE, square) * rest
    half_cosine = horner(COSINE, square)
    return (1.0 - half_sine * half_sine, half_sine * half_cosine)


def cost(flops):
    return pl.CostEstimate(flops=flops, bytes_accessed=flops // 1000, transcendentals=0)


def in_hbm(value):
    return pltpu.with_memory_space_constraint(value, pltpu.HBM)


def pad_up(value, unit):
    return -(-value // unit) * unit


def tails_side_by_side(rows_of, width, tail):
    lane = lax.broadcasted_iota(jnp.int32, (COORD_ROWS, width), 1)
    total = jnp.zeros((COORD_ROWS, width), F32)
    for l, rows in enumerate(rows_of):
        total = jnp.where((lane >= l * tail) & (lane < (l + 1) * tail), rows[:, :width], total)
    return total


def prepare_kernel(
    layer_ref, counts_any, features_any, offsets_any, waves_any, filter_any,
    payload_ref, cols_ref, waves_ref, filter_ref,
    counts_ref, features_ref, offsets_ref, rows_ref, sems,
):
    copies = [
        pltpu.make_async_copy(source, target, sems.at[i])
        for i, (source, target) in enumerate(
            (
                (features_any, features_ref),
                (offsets_any, offsets_ref),
                (counts_any, counts_ref),
                (waves_any, waves_ref),
                (filter_any, filter_ref),
            )
        )
    ]
    for copy in copies:
        copy.start()
    cells, slots, width = features_ref.shape
    atoms = cells * slots
    tail = atoms - width
    slot = lax.broadcasted_iota(jnp.int32, (slots, width), 0)
    lane = lax.broadcasted_iota(jnp.int32, (1, width), 1)
    main_cells = width // slots
    for copy in copies[1:3]:
        copy.wait()
    within = [offsets_ref[cell].astype(F32) for cell in range(cells)]
    for first, parts in (
        (0, list(range(main_cells))),
        (8, list(range(main_cells, cells)) * (width // tail)),
    ):
        along_x = jnp.zeros((1, width), F32)
        along_y = jnp.zeros((1, width), F32)
        lives = jnp.zeros((1, width), jnp.int32)
        for place, cell in enumerate(parts):
            here = (lane >= place * slots) & (lane < (place + 1) * slots)
            along_x = jnp.where(here, float(cell // GRID), along_x)
            along_y = jnp.where(here, float(cell % GRID), along_y)
            lives = jnp.where(here, counts_ref[cell] + place * slots, lives)
        rows_ref[first : first + 1, :] = along_x
        rows_ref[first + 1 : first + 2, :] = along_y
        rows_ref[first + 2 : first + 3, :] = jnp.full((1, width), layer_ref[0].astype(F32))
        rows_ref[first + 3 : first + 6, :] = jnp.concatenate([within[c] for c in parts], axis=1)
        rows_ref[first + 6 : first + 7, :] = jnp.where(lane < lives, 1.0, 0.0)
        rows_ref[first + 7 : first + 8, :] = jnp.zeros((1, width), F32)
    rows = rows_ref[...]
    payload_ref[atoms : atoms + COORD_ROWS, :] = rows.astype(BF16)
    cols_ref[0:width, :] = rows.T
    cols_ref[width:atoms, 0:8] = rows[8:16, 0:LANES].T[0:tail]
    cols_ref[width:atoms, 8:16] = jnp.zeros((tail, 8), F32)
    copies[0].wait()
    for cell in range(cells):
        rows = features_ref[cell].astype(F32)
        payload_ref[cell * slots : (cell + 1) * slots, :] = jnp.where(
            slot < counts_ref[cell], rows, 0.0
        ).astype(BF16)
    for copy in copies[3:]:
        copy.wait()


def prepare(layer, counts, atom_features, offsets, wavevectors, wave_filter):
    cells, slots, width = atom_features.shape
    atoms = cells * slots
    smem = pl.BlockSpec(memory_space=pltpu.SMEM)
    vmem = pl.BlockSpec(memory_space=pltpu.VMEM)
    anywhere = pl.BlockSpec(memory_space=pltpu.HBM)
    return pl.pallas_call(
        prepare_kernel,
        out_shape=(
            jax.ShapeDtypeStruct((atoms + COORD_ROWS, width), BF16),
            jax.ShapeDtypeStruct((atoms, COORD_ROWS), F32),
            jax.ShapeDtypeStruct(wavevectors.shape, wavevectors.dtype),
            jax.ShapeDtypeStruct(wave_filter.shape, wave_filter.dtype),
        ),
        in_specs=[smem] + [anywhere] * 5,
        out_specs=(vmem,) * 4,
        scratch_shapes=[
            pltpu.SMEM(counts.shape, jnp.int32),
            pltpu.VMEM(atom_features.shape, BF16),
            pltpu.VMEM(offsets.shape, BF16),
            pltpu.VMEM((COORD_ROWS, width), F32),
            pltpu.SemaphoreType.DMA((5,)),
        ],
        compiler_params=PARAMS,
        name="prepare",
    )(layer, *map(in_hbm, (counts, atom_features, offsets, wavevectors, wave_filter)))


def wave_kernel(
    size, waves_ref, filter_ref, rows_ref, main_ref, tail_ref, gain_ref, all_ref
):
    wave_count = waves_ref.shape[1]
    basis_count, width = filter_ref.shape
    all_ref[...] = jnp.zeros(all_ref.shape, F32)
    taken = waves_ref[...].astype(F32)
    for first in (0, 3):
        all_ref[first : first + 2, :] = taken[0:2] * (1.0 / GRID)
        all_ref[first + 2 : first + 3, :] = taken[2:3] * (1.0 / size)
    rest = all_ref[...]
    own = rest[0:3] * (2.0 * math.pi)
    terms = []
    for term in range(TERMS):
        rounded = rest.astype(BF16).astype(F32)
        rows_ref[term * COORD_ROWS : (term + 1) * COORD_ROWS, :] = rounded.astype(BF16)
        terms.append(rounded)
        rest = rest - rounded
    main_ref[...] = jnp.concatenate(terms, axis=0).T.astype(BF16)
    tail_ref[...] = jnp.concatenate(
        [rows for term in terms for rows in (term[8:16], term[0:8])], axis=0
    ).T.astype(BF16)
    along_x, along_y, along_z = own[0:1], own[1:2], own[2:3]
    magnitude = jnp.sqrt(along_x * along_x + along_y * along_y + along_z * along_z)
    basis = []
    for b in range(pad_up(basis_count, 8)):
        offset_k = (magnitude - 3.0 * b) * (1.0 / 3.0)
        basis.append(jnp.exp(-(offset_k * offset_k)))
    columns = jnp.concatenate(basis, axis=0).T
    gain = columns[:, 0:1] * filter_ref[0:1, :]
    for b in range(1, basis_count):
        gain = gain + columns[:, b : b + 1] * filter_ref[b : b + 1, :]
    gain_ref[...] = gain


def wave_tables(wavevectors, wave_filter, size):
    wave_count, width = wavevectors.shape[1], wave_filter.shape[1]
    vmem = pl.BlockSpec(memory_space=pltpu.VMEM)
    return pl.pallas_call(
        functools.partial(wave_kernel, size),
        out_shape=(
            jax.ShapeDtypeStruct((TERMS * COORD_ROWS, wave_count), BF16),
            jax.ShapeDtypeStruct((wave_count, TERMS * COORD_ROWS), BF16),
            jax.ShapeDtypeStruct((wave_count, TERMS * COORD_ROWS), BF16),
            jax.ShapeDtypeStruct((wave_count, width), F32),
        ),
        in_specs=[vmem, vmem],
        out_specs=(vmem,) * 4,
        scratch_shapes=[pltpu.VMEM((COORD_ROWS, wave_count), F32)],
        compiler_params=PARAMS,
        name="waves",
    )(wavevectors, wave_filter)


def structure_kernel(chunk_count, atoms, parts, sent, *refs):
    chunks, refs = refs[:chunk_count], refs[chunk_count:]
    main_ref, tail_ref, _, refs = refs[0], refs[1], refs[2], refs[3:]
    count = len(parts)
    sums, outs, refs = refs[:count], refs[count : 2 * count], refs[2 * count :]
    sent_ref = None
    if sent:
        sent_ref, refs = refs[0], refs[1:]
    phases, tables, stack_ref = refs[:count], refs[count : 2 * count], refs[2 * count]
    half = main_ref.shape[0] // 2
    width = chunks[0].shape[1]
    tail = atoms - width
    depth = stack_ref.shape[0]
    split = chunk_count * width
    step = 32
    for l, chunk in enumerate(chunks):
        stack_ref[l * width : (l + 1) * width, :] = chunk[0:width, :]
        at = split + l * tail
        stack_ref[at : at + tail, :] = chunk[width:atoms, :]
    used = chunk_count * atoms
    if used < depth:
        stack_ref[used:depth, :] = jnp.zeros((depth - used, width), BF16)
    rows = tails_side_by_side(
        [chunk[atoms : atoms + COORD_ROWS, :].astype(F32) for chunk in chunks], depth - split, tail
    )
    for part, sum_ref, out_ref, phase_ref, table_ref in zip(parts, sums, outs, phases, tables):
        waves = slice(part * half, (part + 1) * half)
        for l, chunk in enumerate(chunks):
            places = jnp.concatenate([chunk[atoms : atoms + COORD_ROWS, :]] * TERMS, axis=0)
            phase_ref[:, l * width : (l + 1) * width] = jnp.dot(
                main_ref[waves], places, preferred_element_type=F32
            )
        phase_ref[:, split:depth] = jnp.dot(
            tail_ref[waves],
            jnp.concatenate([rows.astype(BF16)] * TERMS, axis=0),
            preferred_element_type=F32,
        )
        for first_lane in range(0, depth, width):
            here = slice(first_lane, min(first_lane + width, depth))
            for row in range(0, half, step):
                cosine, sine = turn_cos_sin(phase_ref[row : row + step, here])
                table_ref[row : row + step, here] = cosine.astype(BF16)
                table_ref[half + row : half + row + step, here] = sine.astype(BF16)
        total = jnp.dot(table_ref[...], stack_ref[...], preferred_element_type=F32) + sum_ref[...]
        out_ref[...] = total
        if sent_ref is not None:
            sent_ref[...] = total.astype(BF16)


def add_structure(chunks, parts, main_waves, tail_waves, token, sums, atoms, sent=False):
    count = len(chunks)
    width = chunks[0].shape[1]
    half = main_waves.shape[0] // 2
    depth = count * width + pad_up(count * (atoms - width), LANES)
    vmem = pl.BlockSpec(memory_space=pltpu.VMEM)
    return pl.pallas_call(
        functools.partial(structure_kernel, count, atoms, parts, sent),
        in_specs=[vmem] * (count + 2) + [pl.BlockSpec(memory_space=pl.ANY)] + [vmem] * len(parts),
        out_specs=[vmem] * (len(parts) + sent),
        out_shape=[jax.ShapeDtypeStruct((2 * half, width), F32)] * len(parts)
        + [jax.ShapeDtypeStruct((2 * half, width), BF16)] * sent,
        scratch_shapes=[pltpu.VMEM((half, depth), F32)] * len(parts)
        + [pltpu.VMEM((2 * half, depth), BF16)] * len(parts)
        + [pltpu.VMEM((depth, width), BF16)],
        compiler_params=PARAMS,
        cost_estimate=cost(12 * half * len(parts) * depth * width),
        name="structure",
    )(*chunks, main_waves, tail_waves, token, *sums)


def own_kernel(cols_ref, waves_ref, payload_ref, table_ref, mine_ref, other_ref, phase_ref):
    waves = waves_ref.shape[1]
    half = waves // 2
    atoms = cols_ref.shape[0]
    places = cols_ref[...].astype(BF16)
    phase_ref[...] = jnp.dot(
        jnp.concatenate([places] * TERMS, axis=1), waves_ref[...], preferred_element_type=F32
    )
    step = 16
    for part, out_ref in enumerate((mine_ref, other_ref)):
        at = part * waves
        for row in range(0, atoms, step):
            cosine, sine = turn_cos_sin(
                phase_ref[row : row + step, part * half : (part + 1) * half]
            )
            table_ref[row : row + step, at : at + half] = cosine.astype(BF16)
            table_ref[row : row + step, at + half : at + waves] = sine.astype(BF16)
        out_ref[...] = lax.dot_general(
            table_ref[:, at : at + waves],
            payload_ref[0:atoms, :],
            (((0,), (0,)), ((), ())),
            preferred_element_type=F32,
        )


def own_layer(own_cols, wave_rows, payload):
    atoms, waves = own_cols.shape[0], wave_rows.shape[1]
    width = payload.shape[1]
    return pl.pallas_call(
        own_kernel,
        out_shape=(
            jax.ShapeDtypeStruct((atoms, 2 * waves), BF16),
            jax.ShapeDtypeStruct((waves, width), F32),
            jax.ShapeDtypeStruct((waves, width), F32),
        ),
        scratch_shapes=[pltpu.VMEM((atoms, waves), F32)],
        compiler_params=PARAMS,
        cost_estimate=cost(4 * atoms * waves * width),
        name="own_layer",
    )(own_cols, wave_rows, payload)


def short_kernel(cells, slots, basis_count, signs, holds_own, last, scale, *refs):
    count = len(signs)
    side_ref, refs = refs[0], refs[1:]
    chunks, refs = refs[:count], refs[count:]
    cols_ref, radial_ref, refs = refs[0], refs[1], refs[2:]
    if last:
        before_ref, features_ref, refs = refs[0], refs[1], refs[2:]
    out_ref, near_ref, weight_ref, mixed_ref = refs
    atoms = cells * slots
    width = chunks[0].shape[1]
    tail = atoms - width
    near = near_ref.shape[0]
    tail_width = near - count * width
    side = side_ref[0].astype(F32)
    shifts = [sign * side for sign in signs]
    mains, tails = [], []
    tail_lane = lax.broadcasted_iota(jnp.int32, (1, tail_width), 1)
    shift_row = jnp.zeros((1, tail_width), F32)
    for l, chunk in enumerate(chunks):
        near_ref[l * width : (l + 1) * width, :] = chunk[0:width, :]
        at = count * width + l * tail
        near_ref[at : at + tail, :] = chunk[width:atoms, :]
        rows = chunk[atoms : atoms + COORD_ROWS, :].astype(F32)
        mains.append((rows[0:1], rows[1:2], rows[3:4], rows[4:5], rows[5:6] + shifts[l]))
        tails.append(rows)
        here = (tail_lane >= l * tail) & (tail_lane < (l + 1) * tail)
        shift_row = jnp.where(here, shifts[l], shift_row)
    used = count * (width + tail)
    if used < near:
        near_ref[used:near, :] = jnp.zeros((near - used, width), BF16)
    joined = tails_side_by_side(tails, tail_width, tail)
    mains.append(
        (joined[8:9], joined[9:10], joined[11:12], joined[12:13], joined[13:14] + shift_row)
    )
    cell_x, cell_y, off_x, off_y, off_z = (
        jnp.concatenate([part[k] for part in mains], axis=1) for k in range(5)
    )
    lane = lax.broadcasted_iota(jnp.int32, (1, near), 1)
    own_index = jnp.where(
        lane < width,
        lane,
        jnp.where(
            (lane >= count * width) & (lane < count * width + tail),
            lane - (count - 1) * width,
            near,
        ),
    )

    def wrapped(delta):
        return jnp.where(
            delta >= GRID - 1.0, delta - GRID, jnp.where(delta < -1.0, delta + GRID, delta)
        )

    step = 16
    sharp = basis_count / CUTOFF
    for cell in range(cells):
        row_x = wrapped(cell_x - float(cell // GRID)) + off_x
        row_y = wrapped(cell_y - float(cell % GRID)) + off_y
        for row in range(cell * slots, (cell + 1) * slots, step):
            own = cols_ref[row : row + step, :]
            delta_x = row_x - own[:, 3:4]
            delta_y = row_y - own[:, 4:5]
            delta_z = off_z - own[:, 5:6]
            square = delta_x * delta_x + delta_y * delta_y + delta_z * delta_z
            root = horner(HALF_COSINE, square * (1.0 / (CUTOFF * CUTOFF)))
            counted = square < CUTOFF * CUTOFF
            if holds_own:
                own_row = row + lax.broadcasted_iota(jnp.int32, (step, 1), 0)
                counted = counted & (own_index != own_row)
            smooth = jnp.where(counted, root * root, 0.0)
            scaled = jnp.sqrt(square) * sharp - 0.5
            weight = jnp.exp(-(scaled * scaled)) * smooth
            growth = jnp.exp(2.0 * scaled)
            for basis in range(basis_count):
                if basis:
                    weight = weight * (growth * math.exp(1.0 - 2.0 * basis))
                weight_ref[basis * atoms + row : basis * atoms + row + step, :] = weight.astype(BF16)
    for basis in range(basis_count):
        mixed_ref[:, basis * width : (basis + 1) * width] = jnp.dot(
            weight_ref[basis * atoms : (basis + 1) * atoms, :],
            near_ref[...],
            preferred_element_type=F32,
        ).astype(BF16)
    total = jnp.dot(mixed_ref[...], radial_ref[...], preferred_element_type=F32)
    if last:
        total = (total + before_ref[...]) * scale + features_ref[0:atoms, :].astype(F32)
    out_ref[...] = total


def short_range(side, chunks, signs, own_cols, radial_flat, slots, basis_count, before=None):
    atoms = own_cols.shape[0]
    count = len(chunks)
    width = chunks[0].shape[1]
    near = count * width + pad_up(count * (atoms - width), LANES)
    last = before is not None
    more = before if last else ()
    vmem = pl.BlockSpec(memory_space=pltpu.VMEM)
    scale = 1.0 / math.sqrt(slots)
    return pl.pallas_call(
        functools.partial(
            short_kernel, atoms // slots, slots, basis_count, signs, not last, last, scale
        ),
        out_shape=jax.ShapeDtypeStruct((atoms, width), F32),
        in_specs=[pl.BlockSpec(memory_space=pltpu.SMEM)] + [vmem] * (count + 2 + len(more)),
        out_specs=vmem,
        scratch_shapes=[
            pltpu.VMEM((near, width), BF16),
            pltpu.VMEM((basis_count * atoms, near), BF16),
            pltpu.VMEM((atoms, basis_count * width), BF16),
        ],
        compiler_params=PARAMS,
        cost_estimate=cost(10 * basis_count * atoms * near * width),
        name="short_range",
    )(side, *chunks, own_cols, radial_flat, *more)


def inverse_kernel(
    part, scale, last, table_ref, mine_ref, other_ref, charge_ref, gain_ref, base_ref, cols_ref,
    out_ref, factor_ref,
):
    waves = mine_ref.shape[0]
    half = waves // 2
    total = mine_ref[...] + other_ref[...].astype(F32)
    structure = jnp.dot(total.astype(BF16), charge_ref[...], preferred_element_type=F32)
    gain = gain_ref[part * half : (part + 1) * half, :]
    factor_ref[0:half] = (structure[0:half] * gain).astype(BF16)
    factor_ref[half:] = (structure[half:] * gain).astype(BF16)
    total = base_ref[...] + scale * jnp.dot(
        table_ref[:, part * waves : (part + 1) * waves],
        factor_ref[...],
        preferred_element_type=F32,
    )
    if not last:
        out_ref[...] = total
        return
    total = jnp.where(cols_ref[:, 6:7] > 0.5, total, 0.0)
    cells, slots, _ = out_ref.shape
    for cell in range(cells):
        out_ref[cell] = total[cell * slots : (cell + 1) * slots].astype(BF16)


def add_inverse(
    part, scale, table, mine, other, charge_weight, gain, base, own_cols, out_shape=None
):
    last = out_shape is not None
    return pl.pallas_call(
        functools.partial(inverse_kernel, part, scale, last),
        out_shape=out_shape if last else jax.ShapeDtypeStruct(base.shape, F32),
        scratch_shapes=[pltpu.VMEM(mine.shape, BF16)],
        compiler_params=PARAMS,
        cost_estimate=cost(mine.shape[0] * mine.shape[1] * base.shape[0] * 4),
        name="inverse",
    )(table, mine, other, charge_weight, gain, base, own_cols)


def local(atom_features, offsets, counts, radial_weight, charge_weight, wave_filter, wavevectors):
    cells, slots, width = atom_features.shape
    atoms = cells * slots
    basis_count = radial_weight.shape[0]
    wave_count = wavevectors.shape[1]
    size = lax.axis_size("space")
    layer = lax.axis_index("space")
    cores = 2 if size % 2 == 0 else 1
    near_y = 2 if (size // cores) % 2 == 0 else 1
    deep = size // (cores * near_y)
    core = layer % cores
    layer_scalar = layer.astype(jnp.int32).reshape(1)
    core_scalar = core.astype(jnp.int32).reshape(1)
    payload, own_cols, own_waves, own_filter = prepare(
        layer_scalar, counts, atom_features, offsets, wavevectors, wave_filter
    )

    def swap(value, mask):
        return lax.ppermute(value, "space", [(i, i ^ mask) for i in range(size)])

    rows_main, main_waves, tail_waves, gain = wave_tables(own_waves, own_filter, size)
    table, *sums = own_layer(own_cols, rows_main, payload)
    side = 1 - 2 * core_scalar
    radial_flat = radial_weight.reshape(basis_count * width, width)

    stride = cores * near_y
    near_keys = [k for k in range(1, deep) if k == 1]
    far_keys = [k for k in range(deep - 1, 2, -1)]
    last_keys = [k for k in range(1, deep) if k == 2]
    along = {k: swap(payload, k * stride) for k in far_keys}
    along.update({k: swap(payload, k * stride) for k in near_keys})
    beside = swap(payload, cores)
    pair = swap(payload, 1)

    def structure(chunks, parts, token, sums, sent=False):
        groups = [chunks[i : i + 4] for i in range(0, len(chunks), 4)]
        for index, group in enumerate(groups):
            ends = sent and index == len(groups) - 1
            sums = add_structure(
                group, parts, main_waves, tail_waves, token, sums, atoms, ends
            )
        return sums

    def after(value, token):
        return lax.optimization_barrier((value, token))[0]

    both = (0, 1)
    across = {k: swap(after(along[k], table), cores) for k in near_keys}
    sums = structure([beside] + [along[k] for k in near_keys], both, side, sums)
    short = short_range(side, (payload, pair), (0.0, 1.0), own_cols, radial_flat, slots, basis_count)
    along.update({k: swap(after(payload, short), k * stride) for k in last_keys})
    near = dict(across)
    for k in far_keys:
        across[k] = swap(after(along[k], (sums[1], short)), cores)
    sums = structure(
        [along[k] for k in far_keys] + [across[k] for k in near_keys], both, short, sums
    )
    for k in last_keys:
        across[k] = swap(after(along[k], sums[1]), cores)

    z = layer // stride
    y = (layer // cores) % near_y
    step_z = jnp.where(core == 0, 1, deep - 1)
    wanted = z ^ ((z + step_z) % deep)
    crossing = beside
    for k in across:
        if k & (k + 1) == 0:
            take = (wanted == k) & (y == jnp.where(core == 0, near_y - 1, 0))
            crossing = jnp.where(take, across[k], crossing)
    far = swap(crossing, 1)
    sums = structure([along[k] for k in last_keys] + [across[k] for k in far_keys], both, side, sums)
    base = short_range(
        side, (far,), (-1.0,), own_cols, radial_flat, slots, basis_count, (short, payload)
    )
    final = [across[k] for k in last_keys]
    mine_a, sent_a = structure(final, (0,), base, sums[:1], True)
    mine_b, sent_b = structure(final, (1,), sent_a, sums[1:], True)
    theirs_a = swap(sent_a, 1)
    theirs_b = swap(sent_b, 1)

    recip_scale = 1.0 / math.sqrt(atoms * size * wave_count)
    base = add_inverse(0, recip_scale, table, mine_a, theirs_a, charge_weight, gain, base, own_cols)
    out_shape = jax.ShapeDtypeStruct(atom_features.shape, BF16)
    return add_inverse(
        1, recip_scale, table, mine_b, theirs_b, charge_weight, gain, base, own_cols, out_shape
    )


def solution(mesh):
    in_specs = (
        P(("groups", "space"), None, None),
        P(("groups", "space"), None, None),
        P(("groups", "space")),
        P(),
        P(),
        P(),
        P(),
    )
    out_specs = P(("groups", "space"), None, None)
    return jax.shard_map(local, mesh=mesh, in_specs=in_specs, out_specs=out_specs, check_vma=False)
```

```python
import functools
import math

import jax
import jax.numpy as jnp
from jax import lax
from jax.experimental import pallas as pl
from jax.experimental.pallas import tpu as pltpu
from jax.sharding import PartitionSpec as P

GRID = 3
CUTOFF = 1.0
BF16 = jnp.bfloat16
F32 = jnp.float32
COORD_ROWS = 16
LANES = 128
TERMS = 3
SINE = (4.44287959, -7.30781805, 3.59778873, -0.791238217)
COSINE = (1.41420408, -6.97764206, 5.7152384, -1.72834866)
HALF_COSINE = (0.999999953, -1.23369821, 0.253650745, -0.0208106275, 0.000858190619)
PARAMS = pltpu.CompilerParams(vmem_limit_bytes=32 * 1024 * 1024)
WIDE = pltpu.CompilerParams(vmem_limit_bytes=62 * 1024 * 1024)


def horner(coefficients, value):
    total = coefficients[-1]
    for coefficient in coefficients[-2::-1]:
        total = total * value + coefficient
    return total


def turn_cos_sin(turns):
    rest = turns - jnp.round(turns)
    square = rest * rest
    half_sine = horner(SINE, square) * rest
    half_cosine = horner(COSINE, square)
    return (1.0 - half_sine * half_sine, half_sine * half_cosine)


def cost(flops):
    return pl.CostEstimate(flops=flops, bytes_accessed=flops // 1000, transcendentals=0)


def in_hbm(value):
    return pltpu.with_memory_space_constraint(value, pltpu.HBM)


def pad_up(value, unit):
    return -(-value // unit) * unit


def tails_side_by_side(rows_of, width, tail):
    lane = lax.broadcasted_iota(jnp.int32, (COORD_ROWS, width), 1)
    total = jnp.zeros((COORD_ROWS, width), F32)
    for l, rows in enumerate(rows_of):
        total = jnp.where((lane >= l * tail) & (lane < (l + 1) * tail), rows[:, :width], total)
    return total


def prepare_kernel(
    layer_ref, counts_any, features_any, offsets_any, waves_any, filter_any,
    payload_ref, cols_ref, waves_ref, filter_ref,
    counts_ref, features_ref, offsets_ref, rows_ref, sems,
):
    copies = [
        pltpu.make_async_copy(source, target, sems.at[i])
        for i, (source, target) in enumerate(
            (
                (features_any, features_ref),
                (offsets_any, offsets_ref),
                (counts_any, counts_ref),
                (waves_any, waves_ref),
                (filter_any, filter_ref),
            )
        )
    ]
    for copy in copies:
        copy.start()
    cells, slots, width = features_ref.shape
    atoms = cells * slots
    tail = atoms - width
    slot = lax.broadcasted_iota(jnp.int32, (slots, width), 0)
    lane = lax.broadcasted_iota(jnp.int32, (1, width), 1)
    main_cells = width // slots
    for copy in copies[1:3]:
        copy.wait()
    within = [offsets_ref[cell].astype(F32) for cell in range(cells)]
    for first, parts in (
        (0, list(range(main_cells))),
        (8, list(range(main_cells, cells)) * (width // tail)),
    ):
        along_x = jnp.zeros((1, width), F32)
        along_y = jnp.zeros((1, width), F32)
        lives = jnp.zeros((1, width), jnp.int32)
        for place, cell in enumerate(parts):
            here = (lane >= place * slots) & (lane < (place + 1) * slots)
            along_x = jnp.where(here, float(cell // GRID), along_x)
            along_y = jnp.where(here, float(cell % GRID), along_y)
            lives = jnp.where(here, counts_ref[cell] + place * slots, lives)
        rows_ref[first : first + 1, :] = along_x
        rows_ref[first + 1 : first + 2, :] = along_y
        rows_ref[first + 2 : first + 3, :] = jnp.full((1, width), layer_ref[0].astype(F32))
        rows_ref[first + 3 : first + 6, :] = jnp.concatenate([within[c] for c in parts], axis=1)
        rows_ref[first + 6 : first + 7, :] = jnp.where(lane < lives, 1.0, 0.0)
        rows_ref[first + 7 : first + 8, :] = jnp.zeros((1, width), F32)
    rows = rows_ref[...]
    payload_ref[atoms : atoms + COORD_ROWS, :] = rows.astype(BF16)
    cols_ref[0:width, :] = rows.T
    cols_ref[width:atoms, 0:8] = rows[8:16, 0:LANES].T[0:tail]
    cols_ref[width:atoms, 8:16] = jnp.zeros((tail, 8), F32)
    copies[0].wait()
    for cell in range(cells):
        rows = features_ref[cell].astype(F32)
        payload_ref[cell * slots : (cell + 1) * slots, :] = jnp.where(
            slot < counts_ref[cell], rows, 0.0
        ).astype(BF16)
    for copy in copies[3:]:
        copy.wait()


def prepare(layer, counts, atom_features, offsets, wavevectors, wave_filter):
    cells, slots, width = atom_features.shape
    atoms = cells * slots
    smem = pl.BlockSpec(memory_space=pltpu.SMEM)
    vmem = pl.BlockSpec(memory_space=pltpu.VMEM)
    anywhere = pl.BlockSpec(memory_space=pltpu.HBM)
    return pl.pallas_call(
        prepare_kernel,
        out_shape=(
            jax.ShapeDtypeStruct((atoms + COORD_ROWS, width), BF16),
            jax.ShapeDtypeStruct((atoms, COORD_ROWS), F32),
            jax.ShapeDtypeStruct(wavevectors.shape, wavevectors.dtype),
            jax.ShapeDtypeStruct(wave_filter.shape, wave_filter.dtype),
        ),
        in_specs=[smem] + [anywhere] * 5,
        out_specs=(vmem,) * 4,
        scratch_shapes=[
            pltpu.SMEM(counts.shape, jnp.int32),
            pltpu.VMEM(atom_features.shape, BF16),
            pltpu.VMEM(offsets.shape, BF16),
            pltpu.VMEM((COORD_ROWS, width), F32),
            pltpu.SemaphoreType.DMA((5,)),
        ],
        compiler_params=PARAMS,
        name="prepare",
    )(layer, *map(in_hbm, (counts, atom_features, offsets, wavevectors, wave_filter)))


def wave_kernel(
    size, waves_ref, filter_ref, rows_ref, main_ref, tail_ref, gain_ref, all_ref
):
    wave_count = waves_ref.shape[1]
    basis_count, width = filter_ref.shape
    all_ref[...] = jnp.zeros(all_ref.shape, F32)
    taken = waves_ref[...].astype(F32)
    for first in (0, 3):
        all_ref[first : first + 2, :] = taken[0:2] * (1.0 / GRID)
        all_ref[first + 2 : first + 3, :] = taken[2:3] * (1.0 / size)
    rest = all_ref[...]
    own = rest[0:3] * (2.0 * math.pi)
    terms = []
    for term in range(TERMS):
        rounded = rest.astype(BF16).astype(F32)
        rows_ref[term * COORD_ROWS : (term + 1) * COORD_ROWS, :] = rounded.astype(BF16)
        terms.append(rounded)
        rest = rest - rounded
    main_ref[...] = jnp.concatenate(terms, axis=0).T.astype(BF16)
    tail_ref[...] = jnp.concatenate(
        [rows for term in terms for rows in (term[8:16], term[0:8])], axis=0
    ).T.astype(BF16)
    along_x, along_y, along_z = own[0:1], own[1:2], own[2:3]
    magnitude = jnp.sqrt(along_x * along_x + along_y * along_y + along_z * along_z)
    basis = []
    for b in range(pad_up(basis_count, 8)):
        offset_k = (magnitude - 3.0 * b) * (1.0 / 3.0)
        basis.append(jnp.exp(-(offset_k * offset_k)))
    columns = jnp.concatenate(basis, axis=0).T
    gain = columns[:, 0:1] * filter_ref[0:1, :]
    for b in range(1, basis_count):
        gain = gain + columns[:, b : b + 1] * filter_ref[b : b + 1, :]
    gain_ref[...] = gain


def wave_tables(wavevectors, wave_filter, size):
    wave_count, width = wavevectors.shape[1], wave_filter.shape[1]
    vmem = pl.BlockSpec(memory_space=pltpu.VMEM)
    return pl.pallas_call(
        functools.partial(wave_kernel, size),
        out_shape=(
            jax.ShapeDtypeStruct((TERMS * COORD_ROWS, wave_count), BF16),
            jax.ShapeDtypeStruct((wave_count, TERMS * COORD_ROWS), BF16),
            jax.ShapeDtypeStruct((wave_count, TERMS * COORD_ROWS), BF16),
            jax.ShapeDtypeStruct((wave_count, width), F32),
        ),
        in_specs=[vmem, vmem],
        out_specs=(vmem,) * 4,
        scratch_shapes=[pltpu.VMEM((COORD_ROWS, wave_count), F32)],
        compiler_params=PARAMS,
        name="waves",
    )(wavevectors, wave_filter)


def structure_kernel(chunk_count, atoms, parts, sent, *refs):
    chunks, refs = refs[:chunk_count], refs[chunk_count:]
    main_ref, tail_ref, _, refs = refs[0], refs[1], refs[2], refs[3:]
    count = len(parts)
    sums, outs, refs = refs[:count], refs[count : 2 * count], refs[2 * count :]
    sent_ref = None
    if sent:
        sent_ref, refs = refs[0], refs[1:]
    phases, tables, stack_ref = refs[:count], refs[count : 2 * count], refs[2 * count]
    half = main_ref.shape[0] // 2
    width = chunks[0].shape[1]
    tail = atoms - width
    depth = stack_ref.shape[0]
    split = chunk_count * width
    step = 32
    for l, chunk in enumerate(chunks):
        stack_ref[l * width : (l + 1) * width, :] = chunk[0:width, :]
        at = split + l * tail
        stack_ref[at : at + tail, :] = chunk[width:atoms, :]
    used = chunk_count * atoms
    if used < depth:
        stack_ref[used:depth, :] = jnp.zeros((depth - used, width), BF16)
    rows = tails_side_by_side(
        [chunk[atoms : atoms + COORD_ROWS, :].astype(F32) for chunk in chunks], depth - split, tail
    )
    for part, sum_ref, out_ref, phase_ref, table_ref in zip(parts, sums, outs, phases, tables):
        waves = slice(part * half, (part + 1) * half)
        for l, chunk in enumerate(chunks):
            places = jnp.concatenate([chunk[atoms : atoms + COORD_ROWS, :]] * TERMS, axis=0)
            phase_ref[:, l * width : (l + 1) * width] = jnp.dot(
                main_ref[waves], places, preferred_element_type=F32
            )
        phase_ref[:, split:depth] = jnp.dot(
            tail_ref[waves],
            jnp.concatenate([rows.astype(BF16)] * TERMS, axis=0),
            preferred_element_type=F32,
        )
        for first_lane in range(0, depth, width):
            here = slice(first_lane, min(first_lane + width, depth))
            for row in range(0, half, step):
                cosine, sine = turn_cos_sin(phase_ref[row : row + step, here])
                table_ref[row : row + step, here] = cosine.astype(BF16)
                table_ref[half + row : half + row + step, here] = sine.astype(BF16)
        total = jnp.dot(table_ref[...], stack_ref[...], preferred_element_type=F32) + sum_ref[...]
        out_ref[...] = total
        if sent_ref is not None:
            sent_ref[...] = total.astype(BF16)


def add_structure(chunks, parts, main_waves, tail_waves, token, sums, atoms, sent=False):
    count = len(chunks)
    width = chunks[0].shape[1]
    half = main_waves.shape[0] // 2
    depth = count * width + pad_up(count * (atoms - width), LANES)
    vmem = pl.BlockSpec(memory_space=pltpu.VMEM)
    return pl.pallas_call(
        functools.partial(structure_kernel, count, atoms, parts, sent),
        in_specs=[vmem] * (count + 2) + [pl.BlockSpec(memory_space=pl.ANY)] + [vmem] * len(parts),
        out_specs=[vmem] * (len(parts) + sent),
        out_shape=[jax.ShapeDtypeStruct((2 * half, width), F32)] * len(parts)
        + [jax.ShapeDtypeStruct((2 * half, width), BF16)] * sent,
        scratch_shapes=[pltpu.VMEM((half, depth), F32)] * len(parts)
        + [pltpu.VMEM((2 * half, depth), BF16)] * len(parts)
        + [pltpu.VMEM((depth, width), BF16)],
        compiler_params=PARAMS,
        cost_estimate=cost(12 * half * len(parts) * depth * width),
        name="structure",
    )(*chunks, main_waves, tail_waves, token, *sums)


def own_kernel(
    cols_ref, waves_ref, payload_ref, _, table_ref, mine_ref, other_ref, phase_ref
):
    waves = waves_ref.shape[1]
    half = waves // 2
    atoms = cols_ref.shape[0]
    places = cols_ref[...].astype(BF16)
    phase_ref[...] = jnp.dot(
        jnp.concatenate([places] * TERMS, axis=1), waves_ref[...], preferred_element_type=F32
    )
    step = 16
    for part, out_ref in enumerate((mine_ref, other_ref)):
        at = part * waves
        for row in range(0, atoms, step):
            cosine, sine = turn_cos_sin(
                phase_ref[row : row + step, part * half : (part + 1) * half]
            )
            table_ref[row : row + step, at : at + half] = cosine.astype(BF16)
            table_ref[row : row + step, at + half : at + waves] = sine.astype(BF16)
        out_ref[...] = lax.dot_general(
            table_ref[:, at : at + waves],
            payload_ref[0:atoms, :],
            (((0,), (0,)), ((), ())),
            preferred_element_type=F32,
        )


def own_layer(own_cols, wave_rows, payload, token):
    atoms, waves = own_cols.shape[0], wave_rows.shape[1]
    width = payload.shape[1]
    return pl.pallas_call(
        own_kernel,
        out_shape=(
            jax.ShapeDtypeStruct((atoms, 2 * waves), BF16),
            jax.ShapeDtypeStruct((waves, width), F32),
            jax.ShapeDtypeStruct((waves, width), F32),
        ),
        in_specs=[pl.BlockSpec(memory_space=pltpu.VMEM)] * 3 + [pl.BlockSpec(memory_space=pl.ANY)],
        scratch_shapes=[pltpu.VMEM((atoms, waves), F32)],
        compiler_params=PARAMS,
        cost_estimate=cost(4 * atoms * waves * width),
        name="own_layer",
    )(own_cols, wave_rows, payload, token)


def short_kernel(cells, slots, basis_count, signs, holds_own, last, scale, *refs):
    count = len(signs)
    side_ref, refs = refs[0], refs[1:]
    chunks, refs = refs[:count], refs[count:]
    cols_ref, radial_ref, refs = refs[0], refs[1], refs[2:]
    if last:
        before_ref, features_ref, refs = refs[0], refs[1], refs[2:]
    out_ref, near_ref, weight_ref, mixed_ref = refs
    atoms = cells * slots
    width = chunks[0].shape[1]
    tail = atoms - width
    near = near_ref.shape[0]
    tail_width = near - count * width
    side = side_ref[0].astype(F32)
    shifts = [sign * side for sign in signs]
    mains, tails = [], []
    tail_lane = lax.broadcasted_iota(jnp.int32, (1, tail_width), 1)
    shift_row = jnp.zeros((1, tail_width), F32)
    for l, chunk in enumerate(chunks):
        near_ref[l * width : (l + 1) * width, :] = chunk[0:width, :]
        at = count * width + l * tail
        near_ref[at : at + tail, :] = chunk[width:atoms, :]
        rows = chunk[atoms : atoms + COORD_ROWS, :].astype(F32)
        mains.append((rows[0:1], rows[1:2], rows[3:4], rows[4:5], rows[5:6] + shifts[l]))
        tails.append(rows)
        here = (tail_lane >= l * tail) & (tail_lane < (l + 1) * tail)
        shift_row = jnp.where(here, shifts[l], shift_row)
    used = count * (width + tail)
    if used < near:
        near_ref[used:near, :] = jnp.zeros((near - used, width), BF16)
    joined = tails_side_by_side(tails, tail_width, tail)
    mains.append(
        (joined[8:9], joined[9:10], joined[11:12], joined[12:13], joined[13:14] + shift_row)
    )
    cell_x, cell_y, off_x, off_y, off_z = (
        jnp.concatenate([part[k] for part in mains], axis=1) for k in range(5)
    )
    lane = lax.broadcasted_iota(jnp.int32, (1, near), 1)
    own_index = jnp.where(
        lane < width,
        lane,
        jnp.where(
            (lane >= count * width) & (lane < count * width + tail),
            lane - (count - 1) * width,
            near,
        ),
    )

    def wrapped(delta):
        return jnp.where(
            delta >= GRID - 1.0, delta - GRID, jnp.where(delta < -1.0, delta + GRID, delta)
        )

    step = 16
    sharp = basis_count / CUTOFF
    for cell in range(cells):
        row_x = wrapped(cell_x - float(cell // GRID)) + off_x
        row_y = wrapped(cell_y - float(cell % GRID)) + off_y
        for row in range(cell * slots, (cell + 1) * slots, step):
            own = cols_ref[row : row + step, :]
            delta_x = row_x - own[:, 3:4]
            delta_y = row_y - own[:, 4:5]
            delta_z = off_z - own[:, 5:6]
            square = delta_x * delta_x + delta_y * delta_y + delta_z * delta_z
            root = horner(HALF_COSINE, square * (1.0 / (CUTOFF * CUTOFF)))
            counted = square < CUTOFF * CUTOFF
            if holds_own:
                own_row = row + lax.broadcasted_iota(jnp.int32, (step, 1), 0)
                counted = counted & (own_index != own_row)
            smooth = jnp.where(counted, root * root, 0.0)
            scaled = jnp.sqrt(square) * sharp - 0.5
            weight = jnp.exp(-(scaled * scaled)) * smooth
            growth = jnp.exp(2.0 * scaled)
            for basis in range(basis_count):
                if basis:
                    weight = weight * (growth * math.exp(1.0 - 2.0 * basis))
                weight_ref[basis * atoms + row : basis * atoms + row + step, :] = weight.astype(BF16)
    for basis in range(basis_count):
        mixed_ref[:, basis * width : (basis + 1) * width] = jnp.dot(
            weight_ref[basis * atoms : (basis + 1) * atoms, :],
            near_ref[...],
            preferred_element_type=F32,
        ).astype(BF16)
    total = jnp.dot(mixed_ref[...], radial_ref[...], preferred_element_type=F32)
    if last:
        total = (total + before_ref[...]) * scale + features_ref[0:atoms, :].astype(F32)
    out_ref[...] = total


def short_range(side, chunks, signs, own_cols, radial_flat, slots, basis_count, before=None):
    atoms = own_cols.shape[0]
    count = len(chunks)
    width = chunks[0].shape[1]
    near = count * width + pad_up(count * (atoms - width), LANES)
    last = before is not None
    more = before if last else ()
    vmem = pl.BlockSpec(memory_space=pltpu.VMEM)
    scale = 1.0 / math.sqrt(slots)
    return pl.pallas_call(
        functools.partial(
            short_kernel, atoms // slots, slots, basis_count, signs, not last, last, scale
        ),
        out_shape=jax.ShapeDtypeStruct((atoms, width), F32),
        in_specs=[pl.BlockSpec(memory_space=pltpu.SMEM)] + [vmem] * (count + 2 + len(more)),
        out_specs=vmem,
        scratch_shapes=[
            pltpu.VMEM((near, width), BF16),
            pltpu.VMEM((basis_count * atoms, near), BF16),
            pltpu.VMEM((atoms, basis_count * width), BF16),
        ],
        compiler_params=PARAMS,
        cost_estimate=cost(10 * basis_count * atoms * near * width),
        name="short_range",
    )(side, *chunks, own_cols, radial_flat, *more)


def inverse_kernel(
    part, scale, last, table_ref, mine_ref, other_ref, charge_ref, gain_ref, base_ref, cols_ref,
    out_ref, factor_ref,
):
    waves = mine_ref.shape[0]
    half = waves // 2
    total = mine_ref[...] + other_ref[...].astype(F32)
    structure = jnp.dot(total.astype(BF16), charge_ref[...], preferred_element_type=F32)
    gain = gain_ref[part * half : (part + 1) * half, :]
    factor_ref[0:half] = (structure[0:half] * gain).astype(BF16)
    factor_ref[half:] = (structure[half:] * gain).astype(BF16)
    total = base_ref[...] + scale * jnp.dot(
        table_ref[:, part * waves : (part + 1) * waves],
        factor_ref[...],
        preferred_element_type=F32,
    )
    if not last:
        out_ref[...] = total
        return
    total = jnp.where(cols_ref[:, 6:7] > 0.5, total, 0.0)
    cells, slots, _ = out_ref.shape
    for cell in range(cells):
        out_ref[cell] = total[cell * slots : (cell + 1) * slots].astype(BF16)


def add_inverse(
    part, scale, table, mine, other, charge_weight, gain, base, own_cols, out_shape=None
):
    last = out_shape is not None
    return pl.pallas_call(
        functools.partial(inverse_kernel, part, scale, last),
        out_shape=out_shape if last else jax.ShapeDtypeStruct(base.shape, F32),
        scratch_shapes=[pltpu.VMEM(mine.shape, BF16)],
        compiler_params=PARAMS,
        cost_estimate=cost(mine.shape[0] * mine.shape[1] * base.shape[0] * 4),
        name="inverse",
    )(table, mine, other, charge_weight, gain, base, own_cols)


def local(atom_features, offsets, counts, radial_weight, charge_weight, wave_filter, wavevectors):
    cells, slots, width = atom_features.shape
    atoms = cells * slots
    basis_count = radial_weight.shape[0]
    wave_count = wavevectors.shape[1]
    size = lax.axis_size("space")
    layer = lax.axis_index("space")
    cores = 2 if size % 2 == 0 else 1
    near_y = 2 if (size // cores) % 2 == 0 else 1
    deep = size // (cores * near_y)
    core = layer % cores
    layer_scalar = layer.astype(jnp.int32).reshape(1)
    core_scalar = core.astype(jnp.int32).reshape(1)
    payload, own_cols, own_waves, own_filter = prepare(
        layer_scalar, counts, atom_features, offsets, wavevectors, wave_filter
    )

    def swap(value, mask):
        return lax.ppermute(value, "space", [(i, i ^ mask) for i in range(size)])

    rows_main, main_waves, tail_waves, gain = wave_tables(own_waves, own_filter, size)
    side = 1 - 2 * core_scalar
    radial_flat = radial_weight.reshape(basis_count * width, width)

    def after(value, token):
        return lax.optimization_barrier((value, token))[0]

    stride = cores * near_y
    near_keys = [k for k in range(1, deep) if k == 1]
    far_keys = [k for k in range(deep - 1, 2, -1)]
    last_keys = [k for k in range(1, deep) if k == 2]
    along = {k: swap(payload, k * stride) for k in far_keys}
    along.update({k: swap(payload, k * stride) for k in near_keys})
    beside = swap(after(payload, rows_main), cores)
    pair = swap(payload, 1)

    def structure(chunks, parts, token, sums, sent=False):
        groups = [chunks[i : i + 4] for i in range(0, len(chunks), 4)]
        for index, group in enumerate(groups):
            ends = sent and index == len(groups) - 1
            sums = add_structure(
                group, parts, main_waves, tail_waves, token, sums, atoms, ends
            )
        return sums

    short = short_range(side, (payload, pair), (0.0, 1.0), own_cols, radial_flat, slots, basis_count)
    table, *sums = own_layer(own_cols, rows_main, payload, short)
    both = (0, 1)
    across = {k: swap(after(along[k], table), cores) for k in near_keys}
    sums = structure([beside] + [along[k] for k in near_keys], both, side, sums)
    along.update({k: swap(after(payload, short), k * stride) for k in last_keys})
    near = dict(across)
    for k in far_keys:
        across[k] = swap(after(along[k], (sums[1], short)), cores)
    sums = structure(
        [along[k] for k in far_keys] + [across[k] for k in near_keys], both, short, sums
    )
    for k in last_keys:
        across[k] = swap(after(along[k], sums[1]), cores)

    z = layer // stride
    y = (layer // cores) % near_y
    step_z = jnp.where(core == 0, 1, deep - 1)
    wanted = z ^ ((z + step_z) % deep)
    crossing = beside
    for k in across:
        if k & (k + 1) == 0:
            take = (wanted == k) & (y == jnp.where(core == 0, near_y - 1, 0))
            crossing = jnp.where(take, across[k], crossing)
    far = swap(crossing, 1)
    sums = structure([along[k] for k in last_keys] + [across[k] for k in far_keys], both, side, sums)
    base = short_range(
        side, (far,), (-1.0,), own_cols, radial_flat, slots, basis_count, (short, payload)
    )
    final = [across[k] for k in last_keys]
    mine_a, sent_a = structure(final, (0,), base, sums[:1], True)
    mine_b, sent_b = structure(final, (1,), sent_a, sums[1:], True)
    theirs_a = swap(sent_a, 1)
    theirs_b = swap(sent_b, 1)

    recip_scale = 1.0 / math.sqrt(atoms * size * wave_count)
    base = add_inverse(0, recip_scale, table, mine_a, theirs_a, charge_weight, gain, base, own_cols)
    out_shape = jax.ShapeDtypeStruct(atom_features.shape, BF16)
    return add_inverse(
        1, recip_scale, table, mine_b, theirs_b, charge_weight, gain, base, own_cols, out_shape
    )


def solution(mesh):
    in_specs = (
        P(("groups", "space"), None, None),
        P(("groups", "space"), None, None),
        P(("groups", "space")),
        P(),
        P(),
        P(),
        P(),
    )
    out_specs = P(("groups", "space"), None, None)
    return jax.shard_map(local, mesh=mesh, in_specs=in_specs, out_specs=out_specs, check_vma=False)
```
